512 devices in a mesh: dp: 16 (over z_lo, x), expert: 32 (over z_hi, y, core).
Axes of the slice: x: 4, y: 8, z: 8 (z_hi: 2, z_lo: 4; z = z_hi * 4 + z_lo), core: 2. Of those that a mesh axis runs over, the one named last changes fastest.
Arguments:
- tokens: bfloat16 [24576, 1280], P(('dp', 'expert')), may hold values from -6 to 6
- cotangent: bfloat16 [24576, 1280], P(('dp', 'expert')), may hold values from -6 to 6
- chosen_rows: int32 [512, 32, 3], P(('dp', 'expert')), may hold values from 0 to 47, as said below
- combine_weights: float32 [512, 32, 3], P(('dp', 'expert')), may hold values from 0.05 to 1
- up_weight: bfloat16 [32, 1280, 3584], P('expert', None, 'dp'), may hold values from -0.15625 to 0.15625
- down_weight: bfloat16 [32, 3584, 1280], P('expert', 'dp'), may hold values from -0.09375 to 0.09375
- first_up: bfloat16 [32, 1280, 3584], P('expert', None, 'dp'), may hold values from -6 to 6
- first_down: bfloat16 [32, 3584, 1280], P('expert', 'dp'), may hold values from -6 to 6
- second_up: bfloat16 [32, 1280, 3584], P('expert', None, 'dp'), may hold values from 0.0099487305 to 1
- second_down: bfloat16 [32, 3584, 1280], P('expert', 'dp'), may hold values from 0.0099487305 to 1
- layer_index: int32 [1], replicated, may hold values from 16 to 31
Outputs:
- combined: bfloat16 [24576, 1280], P(('dp', 'expert'))
- gate_grad: float32 [512, 32, 3], P(('dp', 'expert'))
- step_up: bfloat16 [32, 1280, 3584], P('expert', None, 'dp')
- step_down: bfloat16 [32, 3584, 1280], P('expert', 'dp')
The draws below stay inside these ranges and needn't reach their ends.
Inputs may be any that keep to these rules, and one draw needn't show every extreme that they name: `chosen_rows`: for each block and each expert the 3 positions are distinct.
All inputs are finite; a program needn't handle non-finite values.
Results may differ from the reference program's by a relative error of at most 0.024.
Values may be sent and summed in bfloat16 or wider, within the bound.
No kernel may reach another device: no remote copies, remote signals or barrier semaphores. Data moves between devices by JAX's collectives and lax.ppermute only.
A program may use at most 64 MiB of HBM per device.

```python
import math
from functools import partial
import jax
import jax.numpy as jnp
from jax import lax

D = 1280
FF = 3584
TOK_DEV = 48
LAYERS = 32
STEP_COUNT = 10
EXPERTS = 32
BLOCKS = 512
TOKENS = 24576
PICKS = 3
SLOTS = 1536
N_DP = 16


def draw_chosen_rows(key, part):
    key = jax.random.fold_in(key, 11)
    scores = jax.random.randint(key, (BLOCKS, EXPERTS, TOK_DEV), 0, 1 << 20, dtype=jnp.int32)
    scores = scores * TOK_DEV + jnp.arange(TOK_DEV, dtype=jnp.int32)
    ranked = jnp.argsort(scores, axis=-1, stable=True)
    return ranked[..., :PICKS].astype(jnp.int32)


def block_scale(key, dims, cuts, smallest, largest):
    def one(position, blocks):
        draws = jax.random.uniform(jax.random.fold_in(jax.random.fold_in(key, 6), position), (blocks,), jnp.float32, smallest / len(cuts), largest / len(cuts))
        return jnp.repeat(jnp.exp(draws), dims[position] // blocks).reshape((-1,) + (1,) * (len(dims) - position - 1))

    gain = one(*cuts[0])
    for cut in cuts[1:]:
        gain = gain * one(*cut)
    return gain


def centred(stream_key, shape, spread, limit, shards=(), kind=jnp.bfloat16):
    loudness = block_scale(stream_key, shape, shards, -0.22, 0.18) if shards else 1.0
    result = jax.random.normal(stream_key, shape, jnp.float32) * spread * loudness
    return jnp.minimum(jnp.maximum(result, -limit), limit).astype(kind)


def setup_inputs(seed: int = 0) -> dict:
    keys = jax.random.split(jax.random.key(seed), 12)
    tokens = centred(keys[0], (TOKENS, D), 1.0, 6.0, ((0, 512),))
    cotangent = centred(keys[1], (TOKENS, D), 1.0, 6.0, ((0, 512),))
    chosen_rows = draw_chosen_rows(jax.random.fold_in(keys[11], 71), 0)
    combine_weights = jnp.clip(jnp.exp(math.log(1.0) - 2.9957323 * jax.random.uniform(keys[3], (BLOCKS, EXPERTS, PICKS), jnp.float32) ** block_scale(keys[3], (BLOCKS, EXPERTS, PICKS), ((0, 512),), -0.2, 0.2)), 0.05, 1.0)
    up_weight = centred(keys[4], (EXPERTS, D, FF), D ** -0.5, 0.15625, ((0, 32), (2, 16)))
    down_weight = centred(keys[5], (EXPERTS, FF, D), FF ** -0.5, 0.09375, ((0, 32), (1, 16)))
    first_up = centred(keys[6], (EXPERTS, D, FF), 1.0, 6.0, ((0, 32), (2, 16)))
    first_down = centred(keys[7], (EXPERTS, FF, D), 1.0, 6.0, ((0, 32), (1, 16)))
    second_up = jnp.clip(jnp.exp(math.log(1.0) - 4.61031033 * jax.random.uniform(keys[8], (EXPERTS, D, FF), jnp.float32) ** block_scale(keys[8], (EXPERTS, D, FF), ((0, 32), (2, 16)), -0.2, 0.2)), 0.0099487305, 1.0).astype(jnp.bfloat16)
    second_down = jnp.clip(jnp.exp(math.log(1.0) - 4.61031033 * jax.random.uniform(keys[9], (EXPERTS, FF, D), jnp.float32) ** block_scale(keys[9], (EXPERTS, FF, D), ((0, 32), (1, 16)), -0.2, 0.2)), 0.0099487305, 1.0).astype(jnp.bfloat16)
    layer_index = jax.random.randint(keys[10], (1,), LAYERS - 16, LAYERS).astype(jnp.int32)
    return {"tokens": tokens, "cotangent": cotangent, "chosen_rows": chosen_rows, "combine_weights": combine_weights, "up_weight": up_weight, "down_weight": down_weight, "first_up": first_up, "first_down": first_down, "second_up": second_up, "second_down": second_down, "layer_index": layer_index}


BETA_ONE = 0.9
BETA_TWO = 0.999
EPSILON = 1e-08
DECAY_RATE = 0.9
WEIGHT_DECAY = 0.1

def activation(values):
    return jax.nn.gelu(values, approximate=False)

def adam_step(gradient, first_moment, second_moment, weight, factor):
    running_mean = BETA_ONE * first_moment.astype(jnp.float32) + (1.0 - BETA_ONE) * gradient
    running_square = BETA_TWO * second_moment.astype(jnp.float32) + (1.0 - BETA_TWO) * gradient * gradient
    mean_hat = running_mean / (1.0 - BETA_ONE ** STEP_COUNT)
    square_hat = running_square / (1.0 - BETA_TWO ** STEP_COUNT)
    update = mean_hat / (jnp.sqrt(square_hat) + EPSILON) + WEIGHT_DECAY * weight.astype(jnp.float32)
    return (factor * update).astype(jnp.bfloat16)

def expert_pass(factor, operands):
    rows_in, grads_in, up_block, down_block, first_u, first_d, second_u, second_d = operands
    pre_act = jnp.dot(rows_in, up_block, preferred_element_type=jnp.float32)
    hidden = activation(pre_act).astype(jnp.bfloat16)
    group = FF // N_DP
    hidden_parts = hidden.reshape(SLOTS, N_DP, group).transpose(1, 0, 2)
    down_parts = down_block.reshape(N_DP, group, D)

    def add_part(total, pieces):
        term = jnp.dot(pieces[0], pieces[1], preferred_element_type=jnp.float32)
        rounded = lax.optimization_barrier(term.astype(jnp.bfloat16))
        return (total + rounded.astype(jnp.float32), None)
    summed, _ = lax.scan(add_part, jnp.zeros((SLOTS, D), jnp.float32), (hidden_parts, down_parts))
    expert_rows = summed.astype(jnp.bfloat16)
    back_hidden = jnp.dot(grads_in, down_block.T, preferred_element_type=jnp.float32)
    _, pull_back = jax.vjp(activation, pre_act)
    back_pre = pull_back(back_hidden)[0].astype(jnp.bfloat16)
    grad_down = jnp.dot(hidden.T, grads_in, preferred_element_type=jnp.float32)
    grad_up = jnp.dot(rows_in.T, back_pre, preferred_element_type=jnp.float32)
    step_up = adam_step(grad_up, first_u, second_u, up_block, factor)
    step_down = adam_step(grad_down, first_d, second_d, down_block, factor)
    return (expert_rows, step_up, step_down)

def reference(tokens, cotangent, chosen_rows, combine_weights, up_weight, down_weight, first_up, first_down, second_up, second_down, layer_index):
    offsets = (jnp.arange(BLOCKS, dtype=jnp.int32) * TOK_DEV)[:, None, None]
    positions = (chosen_rows.astype(jnp.int32) + offsets).reshape(-1)
    picked = tokens[positions].reshape(BLOCKS, EXPERTS, PICKS, D)
    back_rows = cotangent[positions].reshape(BLOCKS, EXPERTS, PICKS, D)
    scaled = (combine_weights[..., None] * back_rows.astype(jnp.float32)).astype(jnp.bfloat16)
    expert_x = picked.transpose(1, 0, 2, 3).reshape(EXPERTS, SLOTS, D)
    expert_g = scaled.transpose(1, 0, 2, 3).reshape(EXPERTS, SLOTS, D)
    exponent = (LAYERS - 1 - layer_index[0]).astype(jnp.float32)
    factor = jnp.power(jnp.float32(DECAY_RATE), exponent)
    expert_rows, step_up, step_down = lax.map(partial(expert_pass, factor), (expert_x, expert_g, up_weight, down_weight, first_up, first_down, second_up, second_down))
    returned = expert_rows.reshape(EXPERTS, BLOCKS, PICKS, D).transpose(1, 0, 2, 3)
    weighted = combine_weights[..., None] * returned.astype(jnp.float32)
    combined = jnp.zeros((TOKENS, D), jnp.float32).at[positions].add(weighted.reshape(-1, D)).astype(jnp.bfloat16)
    gate_grad = lax.optimization_barrier(jnp.sum(back_rows.astype(jnp.float32) * returned.astype(jnp.float32), axis=-1))
    return (combined, gate_grad, step_up, step_down)
```

```python
import jax
import jax.numpy as jnp
from jax import lax
from jax.sharding import PartitionSpec as P

LAYERS = 32
STEP_COUNT = 10

BETA_ONE = 0.9
BETA_TWO = 0.999
EPSILON = 1e-08
DECAY_RATE = 0.9
WEIGHT_DECAY = 0.1

LINE = 4
RING = 4


def activation(values):
    return jax.nn.gelu(values, approximate=False)


def adam_step(gradient, first_moment, second_moment, weight, factor):
    running_mean = BETA_ONE * first_moment.astype(jnp.float32) + (1.0 - BETA_ONE) * gradient
    running_square = (
        BETA_TWO * second_moment.astype(jnp.float32) + (1.0 - BETA_TWO) * gradient * gradient
    )
    mean_hat = running_mean / (1.0 - BETA_ONE**STEP_COUNT)
    square_hat = running_square / (1.0 - BETA_TWO**STEP_COUNT)
    update = mean_hat / (jnp.sqrt(square_hat) + EPSILON) + WEIGHT_DECAY * weight.astype(jnp.float32)
    return (factor * update).astype(jnp.bfloat16)


def shift(values, along_z, along_x):
    pairs = []
    for z in range(LINE):
        for x in range(RING):
            target = (z + along_z) % LINE * RING + (x + along_x) % RING
            pairs.append((z * RING + x, target))
    return lax.ppermute(values, "dp", pairs)


def exchange(rows):
    return lax.all_to_all(rows, "expert", split_axis=0, concat_axis=0, tiled=True)


def contract(left, right, dims):
    return lax.dot_general(left, right, (dims, ((), ())), preferred_element_type=jnp.float32)


def per_device(
    tokens,
    cotangent,
    chosen_rows,
    combine_weights,
    up_weight,
    down_weight,
    first_up,
    first_down,
    second_up,
    second_down,
    layer_index,
):
    chosen = chosen_rows[0]
    gate_local = combine_weights[0]
    experts, picks = chosen.shape
    width = tokens.shape[1]
    slots = experts * picks
    up_own = up_weight[0].T
    down_own = down_weight[0]
    group = down_own.shape[0]

    own = jnp.concatenate([up_own, down_own])
    left = shift(own, 0, 1)
    right = shift(own, 0, -1)
    up_far = shift(left[:group], 0, 1)
    down_far = shift(right[group:], 0, -1)
    up_all = jnp.concatenate([up_own, left[:group], right[:group], up_far])
    down_all = jnp.concatenate([down_own, left[group:], right[group:], down_far])

    token_rows = tokens[chosen]
    back_rows = cotangent[chosen]
    scaled = (gate_local[..., None] * back_rows.astype(jnp.float32)).astype(jnp.bfloat16)
    rows_own = exchange(token_rows).reshape(slots, width)
    rows_in = jnp.concatenate([rows_own] + [shift(rows_own, -k, 0) for k in range(1, LINE)])
    rows_own, scaled = lax.optimization_barrier((rows_own, scaled))
    grads_own = exchange(scaled).reshape(slots, width)
    rows_in, grads_own = lax.optimization_barrier((rows_in, grads_own))
    grads_in = jnp.concatenate([grads_own] + [shift(grads_own, -k, 0) for k in range(1, LINE)])

    pre_act = contract(rows_in, up_all, ((1,), (1,)))
    hidden = activation(pre_act).astype(jnp.bfloat16)
    partial = contract(hidden, down_all, ((1,), (0,))).astype(jnp.bfloat16)
    parts = partial.reshape(LINE, slots, width)
    total = parts[0].astype(jnp.float32)
    for k in range(1, LINE):
        total = total + shift(parts[k], k, 0).astype(jnp.float32)
    expert_rows = total.astype(jnp.bfloat16).reshape(experts, picks, width)

    back_hidden = contract(grads_in, down_all, ((1,), (1,)))
    _, pull_back = jax.vjp(activation, pre_act)
    back_pre = pull_back(back_hidden)[0].astype(jnp.bfloat16)
    grad_down = contract(hidden, grads_in, ((0,), (0,)))
    grad_up = contract(back_pre, rows_in, ((0,), (0,)))

    def pieces(gradient):
        return [gradient[i * group : (i + 1) * group] for i in range(RING)]

    up_parts, down_parts = pieces(grad_up), pieces(grad_down)
    up_two = shift(up_parts[3].astype(jnp.bfloat16), 0, 1).astype(jnp.float32)
    down_two = shift(down_parts[3].astype(jnp.bfloat16), 0, -1).astype(jnp.float32)
    to_right = jnp.concatenate([up_parts[2] + up_two, down_parts[2]]).astype(jnp.bfloat16)
    to_left = jnp.concatenate([up_parts[1], down_parts[1] + down_two]).astype(jnp.bfloat16)
    expert_rows, to_right, to_left = lax.optimization_barrier((expert_rows, to_right, to_left))
    from_left = shift(to_right, 0, 1).astype(jnp.float32)
    from_right = shift(to_left, 0, -1).astype(jnp.float32)
    total_up = up_parts[0] + from_left[:group] + from_right[:group]
    total_down = down_parts[0] + from_left[group:] + from_right[group:]

    exponent = (LAYERS - 1 - layer_index[0]).astype(jnp.float32)
    factor = jnp.power(jnp.float32(DECAY_RATE), exponent)
    step_up = adam_step(total_up, first_up[0].T, second_up[0].T, up_own, factor).T[None]
    step_down = adam_step(total_down, first_down[0], second_down[0], down_own, factor)[None]

    returned = exchange(expert_rows)
    flat_rows = returned.reshape(slots, width).astype(jnp.float32)
    local_ids = jnp.arange(tokens.shape[0], dtype=jnp.int32)
    one_hot = (chosen.reshape(-1)[None, :] == local_ids[:, None]).astype(jnp.float32)
    combined = jnp.dot(
        one_hot * gate_local.reshape(-1)[None, :],
        flat_rows,
        precision=lax.Precision.HIGHEST,
        preferred_element_type=jnp.float32,
    ).astype(jnp.bfloat16)
    gate_grad = jnp.sum(back_rows.astype(jnp.float32) * returned.astype(jnp.float32), axis=-1)[None]
    return (combined, gate_grad, step_up, step_down)


def solution(mesh):
    placed = (
        P(("dp", "expert"), None),
        P(("dp", "expert"), None),
        P(("dp", "expert"), None, None),
        P(("dp", "expert"), None, None),
        P("expert", None, "dp"),
        P("expert", "dp", None),
        P("expert", None, "dp"),
        P("expert", "dp", None),
        P("expert", None, "dp"),
        P("expert", "dp", None),
        P(),
    )
    return jax.shard_map(
        per_device,
        mesh=mesh,
        in_specs=placed,
        out_specs=(
            P(("dp", "expert"), None),
            P(("dp", "expert"), None, None),
            P("expert", None, "dp"),
            P("expert", "dp", None),
        ),
        check_vma=False,
    )
```

```python
import jax
import jax.numpy as jnp
from jax import lax
from jax.experimental import pallas as pl
from jax.experimental.pallas import tpu as pltpu
from jax.sharding import Mesh, PartitionSpec as P

LAYERS = 32
STEP_COUNT = 10

BETA_ONE = 0.9
BETA_TWO = 0.999
EPSILON = 1e-08
DECAY_RATE = 0.9
WEIGHT_DECAY = 0.1

RING = 4
COLUMN = 8
SOURCES = 16
PICKS = 3
EXPERTS = 32
FROM_ONE = 6
PADDED = 8
CHUNK = SOURCES * PICKS
WIDTH = 1280
GROUP = 224
ROWS = COLUMN * CHUNK
SMALL, LARGE = 12 * 1024 * 1024, 60 * 1024 * 1024


def adam_step(gradient, first_moment, second_moment, weight, factor):
    running_mean = BETA_ONE * first_moment.astype(jnp.float32) + (1.0 - BETA_ONE) * gradient
    running_square = (
        BETA_TWO * second_moment.astype(jnp.float32) + (1.0 - BETA_TWO) * gradient * gradient
    )
    mean_hat = running_mean * (1.0 / (1.0 - BETA_ONE**STEP_COUNT))
    square_hat = running_square * (1.0 / (1.0 - BETA_TWO**STEP_COUNT))
    update = mean_hat / (jnp.sqrt(square_hat) + EPSILON) + WEIGHT_DECAY * weight.astype(jnp.float32)
    return (factor * update).astype(jnp.bfloat16)


def contract(left, right, left_dim, right_dim, precision=None):
    return lax.dot_general(
        left,
        right,
        (((left_dim,), (right_dim,)), ((), ())),
        precision=precision,
        preferred_element_type=jnp.float32,
    )


def call(kernel, shapes, args, scratch=(), flops=0, limit=SMALL, outside=(), outputs_outside=False):
    spec = pl.BlockSpec(memory_space=pltpu.VMEM)
    moved = sum(a.size * a.dtype.itemsize for a in args)
    moved += sum(s.size * s.dtype.itemsize for s in shapes)
    far = pl.BlockSpec(memory_space=pl.ANY)
    scalar = pl.BlockSpec(memory_space=pltpu.SMEM)
    return pl.pallas_call(
        kernel,
        out_shape=shapes,
        in_specs=[
            scalar if a.ndim == 1 else far if i in outside else spec for i, a in enumerate(args)
        ],
        out_specs=[far if outputs_outside else spec] * len(shapes),
        scratch_shapes=scratch,
        compiler_params=pltpu.CompilerParams(vmem_limit_bytes=limit),
        cost_estimate=pl.CostEstimate(flops=flops, bytes_accessed=moved, transcendentals=0),
    )(*args)


def slot_masks():
    shape = (SOURCES * PADDED, EXPERTS)
    row = lax.broadcasted_iota(jnp.int32, shape, 0)
    lane = lax.broadcasted_iota(jnp.int32, shape, 1)
    slot = row & 7
    half = jnp.where(slot >= PICKS, 1, 0)
    same = (lane == half * SOURCES + (row >> 3)) & (slot < FROM_ONE)
    return [same & (slot - PICKS * half == k) for k in range(PICKS)]


def row_values(masks, values_ref):
    column = None
    for k in range(PICKS):
        term = jnp.where(masks[k], values_ref[k].astype(jnp.float32), 0.0)
        term = jnp.sum(term, axis=1, keepdims=True)
        column = term if column is None else column + term
    return column


def row_choice(masks, chosen_ref, tokens):
    chosen = row_values(masks, chosen_ref).astype(jnp.int32)
    local = lax.broadcasted_iota(jnp.int32, (SOURCES * PADDED, tokens), 1)
    return chosen == local


def pick_kernel(tokens, cotangent, chosen, gates, send, token_rows, back_rows, sems):
    copies = [
        pltpu.make_async_copy(tokens, token_rows, sems.at[0]),
        pltpu.make_async_copy(cotangent, back_rows, sems.at[1]),
    ]
    for copy in copies:
        copy.start()
    masks = slot_masks()
    choice = row_choice(masks, chosen, tokens.shape[0]).astype(jnp.bfloat16)
    gate = row_values(masks, gates)
    copies[0].wait()
    picked = contract(choice, token_rows[...], 1, 0)
    copies[1].wait()
    scaled = gate * contract(choice, back_rows[...], 1, 0)
    for i in range(SOURCES):
        here = slice(i * PADDED, i * PADDED + FROM_ONE)
        send[i, :FROM_ONE] = picked[here].astype(jnp.bfloat16)
        send[i, FROM_ONE:] = scaled[here].astype(jnp.bfloat16)


def spread_kernel(place, arrived, *rest):
    sends, (rows, halves) = rest[:4], rest[4:]
    rows[...] = jnp.zeros_like(rows)
    for i in range(SOURCES):
        rows[i * 16 : i * 16 + 2 * FROM_ONE, :] = arrived[i]
    shape = (2 * CHUNK, SOURCES * 16)
    after = lax.broadcasted_iota(jnp.int32, shape, 0)
    before = lax.broadcasted_iota(jnp.int32, shape, 1)
    second = jnp.where(after >= CHUNK, 1, 0)
    after = after - CHUNK * second
    slot = (before & 15) - FROM_ONE * second - (after >> 4)
    for half in range(2):
        order = ((before >> 4) == (after & 15)) & (slot == PICKS * half)
        ordered = contract(order.astype(jnp.bfloat16), rows[...], 1, 0)
        halves[half] = ordered.astype(jnp.bfloat16)
    for send, target in zip(sends, (place[0], place[1], place[2], place[3])):
        send[...] = halves[target >> 2]


def gather_kernel(arrived, send, total):
    for half in range(2):
        chunk = arrived[half].astype(jnp.float32)
        for z in range(1, 4):
            chunk = chunk + arrived[z * 2 + half].astype(jnp.float32)
        total[half * CHUNK : half * CHUNK + CHUNK, :] = chunk.astype(jnp.bfloat16)
    shape = (SOURCES * PADDED, 2 * CHUNK)
    after = lax.broadcasted_iota(jnp.int32, shape, 0)
    before = lax.broadcasted_iota(jnp.int32, shape, 1)
    half = jnp.where(before >= CHUNK, 1, 0)
    before = before - CHUNK * half
    order = ((before & 15) == (after >> 3)) & ((after & 7) == PICKS * half + (before >> 4))
    ordered = contract(order.astype(jnp.bfloat16), total[...], 1, 0)
    for i in range(SOURCES):
        send[i] = ordered[i * PADDED : i * PADDED + FROM_ONE].astype(jnp.bfloat16)


def expert_kernel(place, *args):
    blocks, (own, left, right, up_far, down_far) = args[:8], args[8:13]
    outs, args = args[13:22], args[22:]
    staged, (rows, grads, up, down, units, slopes, sems, out_sems) = args[:9], args[9:]
    halves = pl.ds(0, GROUP), pl.ds(GROUP, GROUP)
    pairs = [(b.at[pl.ds(0, CHUNK)], rows.at[pl.ds(j * CHUNK, CHUNK)]) for j, b in enumerate(blocks)]
    pairs += [(piece.at[halves[0]], up.at[i]) for i, piece in enumerate((own, left, right), 1)]
    pairs += [(up_far, up.at[0])]
    pairs += [(piece.at[halves[1]], down.at[i]) for i, piece in enumerate((own, left, right), 1)]
    pairs += [(down_far, down.at[0])]
    pairs += [
        (b.at[pl.ds(CHUNK, CHUNK)], grads.at[pl.ds(j * CHUNK, CHUNK)]) for j, b in enumerate(blocks)
    ]
    copies = [pltpu.make_async_copy(src, dst, sems.at[n]) for n, (src, dst) in enumerate(pairs)]
    for copy in copies:
        copy.start()
    for copy in copies[:12]:
        copy.wait()
    for i in range(RING):
        pre = contract(up[i], rows[...], 1, 1)
        share = 0.5 * (1.0 + lax.erf(pre * 0.7071067811865476))
        units[i] = (pre * share).astype(jnp.bfloat16)
        slopes[i] = share + pre * (0.3989422804014327 * jnp.exp(-0.5 * pre * pre))
    for copy in copies[12:]:
        copy.wait()
    cuts = [pl.ds(n, 256) for n in range(0, WIDTH, 256)]
    writes = [pltpu.make_async_copy(s, o, out_sems.at[n]) for n, (s, o) in enumerate(zip(staged, outs))]
    for n, i in enumerate((0, 2, 3, 1)):
        back = (slopes[i] * contract(down[i], grads[...], 1, 1)).astype(jnp.bfloat16)
        for cut in cuts:
            for out, a, b in zip(staged[2 * n : 2 * n + 2], (back, units[i]), (rows, grads)):
                out[:, cut] = contract(a, b[:, cut], 1, 0).astype(out.dtype)
        writes[2 * n].start()
        writes[2 * n + 1].start()
    for cut in cuts:
        total = contract(units[0], down[0, :, cut], 0, 0)
        for i in range(1, RING):
            total = total + contract(units[i], down[i, :, cut], 0, 0)
        for j in range(8):
            staged[8][place[j], :, cut] = total[j * CHUNK : j * CHUNK + CHUNK].astype(jnp.bfloat16)
    writes[8].start()
    for write in writes:
        write.wait()


def combine_kernel(returned, cotangent, chosen, gates, combined, gate_grad, rows):
    tokens = cotangent.shape[0]
    rows[...] = jnp.zeros_like(rows)
    for i in range(SOURCES):
        rows[i * PADDED : i * PADDED + FROM_ONE, :] = returned[i].astype(jnp.float32)
    masks = slot_masks()
    choice = row_choice(masks, chosen, tokens)
    gate = row_values(masks, gates)
    weighted = jnp.where(choice, gate, 0.0)
    combined[...] = contract(weighted, rows[...], 0, 0, lax.Precision.HIGHEST).astype(jnp.bfloat16)
    back = contract(choice.astype(jnp.bfloat16), cotangent[...], 1, 0)
    inner = jnp.sum(back * rows[...], axis=1, keepdims=True)
    for k in range(PICKS):
        gate_grad[k] = jnp.sum(jnp.where(masks[k], inner, 0.0), axis=0, keepdims=True)


def shape(*dims, dtype=jnp.bfloat16):
    return jax.ShapeDtypeStruct(dims, dtype)


def along_x(values, step):
    return lax.ppermute(values, "x", [(i, (i + step) % RING) for i in range(RING)])


def within_z(rows):
    return lax.all_to_all(rows, ("y", "core"), split_axis=0, concat_axis=0, tiled=True)


def along_z(rows):
    return lax.all_to_all(rows, ("zlo", "zhi"), split_axis=0, concat_axis=0, tiled=True)


def rank(z):
    return z % 4 * 2 + z // 4


def mate(z):
    return z + 1 - 2 * (z % 2)


def to_chip(rows, target):
    pairs = [(rank(z), rank(target(z) % COLUMN)) for z in range(COLUMN)]
    return lax.ppermute(rows, ("zlo", "zhi"), pairs)


HOPS = (
    lambda z: z + 2 - 4 * (z % 2),
    lambda z: z - 1 + 2 * (z % 2),
    lambda z: z - 3 + 6 * (z % 2),
)
ORIGINS = (lambda z: z - 2 + 4 * (z % 2), HOPS[1], HOPS[2])


def per_device(
    tokens,
    cotangent,
    chosen_rows,
    combine_weights,
    up_weight,
    down_weight,
    first_up,
    first_down,
    second_up,
    second_down,
    layer_index,
):
    chosen = chosen_rows.transpose(2, 0, 1)
    gates = combine_weights.transpose(2, 0, 1)
    up_own = up_weight[0].T
    down_own = down_weight[0]
    f32, bf16 = jnp.float32, jnp.bfloat16

    own = jnp.concatenate([up_own, down_own])
    left = along_x(own, 1)
    right = along_x(own, -1)
    up_far = along_x(left[:GROUP], 1)
    down_far = along_x(right[GROUP:], -1)

    z = (lax.axis_index("zhi") * 4 + lax.axis_index("zlo")).astype(jnp.int32)
    first = [z] + [hop(z) % COLUMN for hop in HOPS]
    sources = [z] + [origin(z) for origin in ORIGINS]
    sources += [mate(z)] + [origin(mate(z)) for origin in ORIGINS]
    slots = jnp.stack([rank(source % COLUMN) for source in sources])
    (send,) = call(
        pick_kernel,
        [shape(SOURCES, 2 * FROM_ONE, WIDTH)],
        [tokens, cotangent, chosen, gates],
        [pltpu.VMEM(tokens.shape, bf16)] * 2 + [pltpu.SemaphoreType.DMA((2,))],
        outside=(0, 1),
    )
    blocks = call(
        spread_kernel,
        [shape(2 * CHUNK, WIDTH)] * 4,
        [jnp.stack(first), within_z(send)],
        [pltpu.VMEM((SOURCES * 16, WIDTH), bf16), pltpu.VMEM((2, 2 * CHUNK, WIDTH), bf16)],
    )
    blocks = [blocks[0]] + [to_chip(block, hop) for block, hop in zip(blocks[1:], HOPS)]
    blocks += [to_chip(block, mate) for block in blocks]

    weight = shape(GROUP, WIDTH)
    wide = shape(GROUP, WIDTH, dtype=f32)
    gradients = [weight, weight, weight, wide, wide, weight, wide, wide]
    results = [*gradients, shape(COLUMN, CHUNK, WIDTH)]
    outputs = call(
        expert_kernel,
        results,
        [slots, *blocks, own, left, right, up_far, down_far],
        [pltpu.VMEM(r.shape, r.dtype) for r in results]
        + [pltpu.VMEM((ROWS, WIDTH), bf16)] * 2
        + [pltpu.VMEM((RING, GROUP, WIDTH), bf16)] * 2
        + [pltpu.VMEM((RING, GROUP, ROWS), dtype) for dtype in (bf16, f32)]
        + [pltpu.SemaphoreType.DMA((24,)), pltpu.SemaphoreType.DMA((9,))],
        flops=40 * ROWS * GROUP * WIDTH,
        limit=LARGE,
        outside=range(1, 14),
        outputs_outside=True,
    )
    far_up, far_down, left_up, left_down, right_up, right_down, own_up, own_down, partial = outputs
    arrived = along_z(partial)

    up_two = along_x(far_up, 1).astype(f32)
    down_two = along_x(far_down, -1).astype(f32)
    up_from_right = along_x(left_up, -1).astype(f32)
    down_from_left = along_x(right_down, 1).astype(f32)
    up_from_left = along_x((right_up + up_two).astype(jnp.bfloat16), 1).astype(f32)
    down_from_right = along_x((left_down + down_two).astype(jnp.bfloat16), -1).astype(f32)
    total_up = own_up + up_from_right + up_from_left
    total_down = own_down + down_from_left + down_from_right

    exponent = (LAYERS - 1 - layer_index[0]).astype(f32)
    factor = jnp.power(f32(DECAY_RATE), exponent)
    step_up = adam_step(total_up, first_up[0].T, second_up[0].T, up_own, factor).T[None]
    step_down = adam_step(total_down, first_down[0], second_down[0], down_own, factor)[None]

    scratch = [pltpu.VMEM((2 * CHUNK, WIDTH), bf16)]
    (summed,) = call(gather_kernel, [shape(SOURCES, FROM_ONE, WIDTH)], [arrived], scratch)
    combined, gate_grad = call(
        combine_kernel,
        [shape(tokens.shape[0], WIDTH), shape(PICKS, 1, EXPERTS, dtype=f32)],
        [within_z(summed), cotangent, chosen, gates],
        [pltpu.VMEM((SOURCES * PADDED, WIDTH), f32)],
    )
    return (combined, gate_grad.transpose(1, 2, 0), step_up, step_down)


def solution(mesh):
    fine = Mesh(mesh.devices.reshape(4, RING, 2, 8, 2), ("zlo", "x", "zhi", "y", "core"))
    dp, expert = ("zlo", "x"), ("zhi", "y", "core")
    both = dp + expert
    placed = (
        P(both, None),
        P(both, None),
        P(both, None, None),
        P(both, None, None),
        P(expert, None, dp),
        P(expert, dp, None),
        P(expert, None, dp),
        P(expert, dp, None),
        P(expert, None, dp),
        P(expert, dp, None),
        P(),
    )
    return jax.shard_map(
        per_device,
        mesh=fine,
        in_specs=placed,
        out_specs=(P(both, None), P(both, None, None), P(expert, None, dp), P(expert, dp, None)),
        check_vma=False,
    )
```

```python
import jax
import jax.numpy as jnp
from jax import lax
from jax.experimental import pallas as pl
from jax.experimental.pallas import tpu as pltpu
from jax.sharding import Mesh, PartitionSpec as P

LAYERS = 32
STEP_COUNT = 10

BETA_ONE = 0.9
BETA_TWO = 0.999
EPSILON = 1e-08
DECAY_RATE = 0.9
WEIGHT_DECAY = 0.1

RING = 4
COLUMN = 8
SOURCES = 16
PICKS = 3
EXPERTS = 32
FROM_ONE = 6
PADDED = 8
CHUNK = SOURCES * PICKS
WIDTH = 1280
GROUP = 224
ROWS = COLUMN * CHUNK
SMALL, LARGE = 12 * 1024 * 1024, 60 * 1024 * 1024


def adam_step(gradient, first_moment, second_moment, weight, factor):
    running_mean = BETA_ONE * first_moment.astype(jnp.float32) + (1.0 - BETA_ONE) * gradient
    running_square = (
        BETA_TWO * second_moment.astype(jnp.float32) + (1.0 - BETA_TWO) * gradient * gradient
    )
    mean_hat = running_mean * (1.0 / (1.0 - BETA_ONE**STEP_COUNT))
    square_hat = running_square * (1.0 / (1.0 - BETA_TWO**STEP_COUNT))
    update = mean_hat / (jnp.sqrt(square_hat) + EPSILON) + WEIGHT_DECAY * weight.astype(jnp.float32)
    return (factor * update).astype(jnp.bfloat16)


def contract(left, right, left_dim, right_dim, precision=None):
    return lax.dot_general(
        left,
        right,
        (((left_dim,), (right_dim,)), ((), ())),
        precision=precision,
        preferred_element_type=jnp.float32,
    )


def call(kernel, shapes, args, scratch=(), flops=0, limit=SMALL, outside=(), outputs_outside=False):
    spec = pl.BlockSpec(memory_space=pltpu.VMEM)
    moved = sum(a.size * a.dtype.itemsize for a in args)
    moved += sum(s.size * s.dtype.itemsize for s in shapes)
    far = pl.BlockSpec(memory_space=pl.ANY)
    scalar = pl.BlockSpec(memory_space=pltpu.SMEM)
    return pl.pallas_call(
        kernel,
        out_shape=shapes,
        in_specs=[
            scalar if a.ndim == 1 else far if i in outside else spec for i, a in enumerate(args)
        ],
        out_specs=[far if outputs_outside else spec] * len(shapes),
        scratch_shapes=scratch,
        compiler_params=pltpu.CompilerParams(vmem_limit_bytes=limit),
        cost_estimate=pl.CostEstimate(flops=flops, bytes_accessed=moved, transcendentals=0),
    )(*args)


def slot_masks():
    shape = (SOURCES * PADDED, EXPERTS)
    row = lax.broadcasted_iota(jnp.int32, shape, 0)
    lane = lax.broadcasted_iota(jnp.int32, shape, 1)
    slot = row & 7
    half = jnp.where(slot >= PICKS, 1, 0)
    same = (lane == half * SOURCES + (row >> 3)) & (slot < FROM_ONE)
    return [same & (slot - PICKS * half == k) for k in range(PICKS)]


def row_values(masks, values_ref):
    column = None
    for k in range(PICKS):
        term = jnp.where(masks[k], values_ref[k].astype(jnp.float32), 0.0)
        term = jnp.sum(term, axis=1, keepdims=True)
        column = term if column is None else column + term
    return column


def row_choice(masks, chosen_ref, tokens):
    chosen = row_values(masks, chosen_ref).astype(jnp.int32)
    local = lax.broadcasted_iota(jnp.int32, (SOURCES * PADDED, tokens), 1)
    return chosen == local


def pick_kernel(tokens, cotangent, chosen, gates, send, token_rows, back_rows, sems):
    copies = [
        pltpu.make_async_copy(tokens, token_rows, sems.at[0]),
        pltpu.make_async_copy(cotangent, back_rows, sems.at[1]),
    ]
    for copy in copies:
        copy.start()
    masks = slot_masks()
    choice = row_choice(masks, chosen, tokens.shape[0]).astype(jnp.bfloat16)
    gate = row_values(masks, gates)
    copies[0].wait()
    picked = contract(choice, token_rows[...], 1, 0)
    copies[1].wait()
    scaled = gate * contract(choice, back_rows[...], 1, 0)
    for i in range(SOURCES):
        here = slice(i * PADDED, i * PADDED + FROM_ONE)
        for n in range(2):
            cut = slice(n * WIDTH // 2, (n + 1) * WIDTH // 2)
            first = 2 * n * FROM_ONE
            send[i, first : first + FROM_ONE] = picked[here, cut].astype(jnp.bfloat16)
            send[i, first + FROM_ONE : first + 2 * FROM_ONE] = scaled[here, cut].astype(jnp.bfloat16)


def spread_kernel(arrived, send, rows):
    rows[...] = jnp.zeros_like(rows)
    for i in range(SOURCES):
        for n in range(2):
            cut = slice(n * WIDTH // 2, (n + 1) * WIDTH // 2)
            part = slice(2 * n * FROM_ONE, 2 * (n + 1) * FROM_ONE)
            rows[i * 16 : i * 16 + 2 * FROM_ONE, cut] = arrived[i, part]
    shape = (2 * CHUNK, SOURCES * 16)
    after = lax.broadcasted_iota(jnp.int32, shape, 0)
    before = lax.broadcasted_iota(jnp.int32, shape, 1)
    second = jnp.where(after >= CHUNK, 1, 0)
    after = after - CHUNK * second
    slot = (before & 15) - FROM_ONE * second - (after >> 4)
    for half in range(2):
        order = ((before >> 4) == (after & 15)) & (slot == PICKS * half)
        ordered = contract(order.astype(jnp.bfloat16), rows[...], 1, 0)
        ordered = ordered.astype(jnp.bfloat16)
        for z in range(4):
            send[z * 2 + half] = ordered


def gather_kernel(arrived, send, total):
    for half in range(2):
        chunk = arrived[half].astype(jnp.float32)
        for z in range(1, 4):
            chunk = chunk + arrived[z * 2 + half].astype(jnp.float32)
        total[half * CHUNK : half * CHUNK + CHUNK, :] = chunk.astype(jnp.bfloat16)
    shape = (SOURCES * PADDED, 2 * CHUNK)
    after = lax.broadcasted_iota(jnp.int32, shape, 0)
    before = lax.broadcasted_iota(jnp.int32, shape, 1)
    half = jnp.where(before >= CHUNK, 1, 0)
    before = before - CHUNK * half
    order = ((before & 15) == (after >> 3)) & ((after & 7) == PICKS * half + (before >> 4))
    ordered = contract(order.astype(jnp.bfloat16), total[...], 1, 0)
    for i in range(SOURCES):
        chunk = ordered[i * PADDED : i * PADDED + FROM_ONE].astype(jnp.bfloat16)
        for n in range(5):
            send[i, n * FROM_ONE : (n + 1) * FROM_ONE] = chunk[:, n * 256 : (n + 1) * 256]


def start_all(pairs, sems, first=0):
    copies = []
    for n, (source, target) in enumerate(pairs, first):
        copies.append(pltpu.make_async_copy(source, target, sems.at[n]))
        copies[-1].start()
    return copies


def wait_all(copies):
    for copy in copies:
        copy.wait()


def row_copies(arrived, half, rows):
    cut = pl.ds(half * CHUNK, CHUNK)
    return [(arrived.at[j, cut], rows.at[pl.ds(j * CHUNK, CHUNK)]) for j in range(COLUMN)]


CUTS = [pl.ds(n, 256) for n in range(0, WIDTH, 256)]


def expert_kernel(arrived, *args):
    ups, downs, outs, staged = args[:4], args[4:8], args[8:17], args[17:26]
    rows, grads, up, down, units, slopes, sems, out_sems = args[26:]
    partial = 8
    pairs = row_copies(arrived, 0, rows)
    pairs += [(ups[i], up.at[i]) for i in range(RING)] + row_copies(arrived, 1, grads)
    pairs += [(downs[i], down.at[i]) for i in range(RING)]
    copies = start_all(pairs, sems)
    wait_all(copies[:COLUMN])
    for i in range(RING):
        copies[COLUMN + i].wait()
        pre = contract(up[i], rows[...], 1, 1)
        share = 0.5 * (1.0 + lax.erf(pre * 0.7071067811865476))
        units[i] = (pre * share).astype(jnp.bfloat16)
        slopes[i] = share + pre * (0.3989422804014327 * jnp.exp(-0.5 * pre * pre))
    wait_all(copies[COLUMN + RING :])
    writes = []
    for i in range(RING):
        back = (slopes[i] * contract(down[i], grads[...], 1, 1)).astype(jnp.bfloat16)
        here = slice(2 * i, 2 * i + 2)
        for cut in CUTS:
            for out, a, b in zip(staged[here], (back, units[i]), (rows, grads)):
                out[:, cut] = contract(a, b[:, cut], 1, 0).astype(jnp.bfloat16)
        writes += start_all(list(zip(staged[here], outs[here])), out_sems, len(writes))
    for cut in CUTS:
        total = contract(units[0], down[0, :, cut], 0, 0)
        for i in range(1, RING):
            total = total + contract(units[i], down[i, :, cut], 0, 0)
        for j in range(COLUMN):
            staged[partial][j, :, cut] = total[j * CHUNK : j * CHUNK + CHUNK].astype(jnp.bfloat16)
    wait_all(writes + start_all([(staged[partial], outs[partial])], out_sems, len(writes)))


def step_kernel(factor, *args):
    sources, outs, (held, staged, sems, out_sems) = args[:12], args[12:14], args[14:]
    parts = [sources[:6], sources[6:]]
    pairs = [(source, held.at[n, m]) for n in range(2) for m, source in enumerate(parts[n])]
    copies = start_all(pairs, sems)
    writes = []
    for n in range(2):
        wait_all(copies[6 * n : 6 * n + 6])
        for start in range(0, GROUP, 32):
            here = pl.ds(start, 32)
            first_moment, second_moment, weight, own, one, two = [held[n, m, here] for m in range(6)]
            gradient = own.astype(jnp.float32) + one.astype(jnp.float32) + two.astype(jnp.float32)
            staged[n, here] = adam_step(gradient, first_moment, second_moment, weight, factor[0])
        writes += start_all([(staged.at[n], outs[n])], out_sems, len(writes))
    wait_all(writes)


def combine_kernel(returned, cotangent, chosen, gates, combined, gate_grad, rows):
    tokens = cotangent.shape[0]
    rows[...] = jnp.zeros_like(rows)
    for i in range(SOURCES):
        for n in range(5):
            part = returned[i, n * FROM_ONE : (n + 1) * FROM_ONE].astype(jnp.float32)
            rows[i * PADDED : i * PADDED + FROM_ONE, n * 256 : (n + 1) * 256] = part
    masks = slot_masks()
    choice = row_choice(masks, chosen, tokens)
    gate = row_values(masks, gates)
    weighted = jnp.where(choice, gate, 0.0)
    combined[...] = contract(weighted, rows[...], 0, 0, lax.Precision.HIGHEST).astype(jnp.bfloat16)
    back = contract(choice.astype(jnp.bfloat16), cotangent[...], 1, 0)
    inner = jnp.sum(back * rows[...], axis=1, keepdims=True)
    for k in range(PICKS):
        gate_grad[k] = jnp.sum(jnp.where(masks[k], inner, 0.0), axis=0, keepdims=True)


def shape(*dims, dtype=jnp.bfloat16):
    return jax.ShapeDtypeStruct(dims, dtype)


def along_x(values, step):
    return lax.ppermute(values, "x", [(i, (i + step) % RING) for i in range(RING)])


def within_z(rows):
    return lax.all_to_all(rows, ("y", "core"), split_axis=0, concat_axis=0, tiled=True)


def along_z(rows):
    return lax.all_to_all(rows, ("zlo", "zhi"), split_axis=0, concat_axis=0, tiled=True)


def per_device(
    tokens,
    cotangent,
    chosen_rows,
    combine_weights,
    up_weight,
    down_weight,
    first_up,
    first_down,
    second_up,
    second_down,
    layer_index,
):
    chosen = chosen_rows.transpose(2, 0, 1)
    gates = combine_weights.transpose(2, 0, 1)
    up_own = up_weight[0].T
    down_own = down_weight[0]
    f32, bf16 = jnp.float32, jnp.bfloat16

    up_left, down_left = along_x(up_own, 1), along_x(down_own, 1)
    up_right, down_right = along_x(up_own, -1), along_x(down_own, -1)

    (send,) = call(
        pick_kernel,
        [shape(SOURCES, 4 * FROM_ONE, WIDTH // 2)],
        [tokens, cotangent, chosen, gates],
        [pltpu.VMEM(tokens.shape, bf16)] * 2 + [pltpu.SemaphoreType.DMA((2,))],
        limit=LARGE,
        outside=(0, 1),
    )
    (spread,) = call(
        spread_kernel,
        [shape(COLUMN, 2 * CHUNK, WIDTH)],
        [within_z(send)],
        [pltpu.VMEM((SOURCES * 16, WIDTH), bf16)],
    )
    rows = along_z(spread)

    ups = [along_x(up_left, 1), up_left, up_right, up_own]
    downs = [along_x(down_right, -1), down_left, down_right, down_own]
    weight = shape(GROUP, WIDTH)
    results = [weight] * 8 + [shape(COLUMN, CHUNK, WIDTH)]
    *gradients, partial = call(
        expert_kernel,
        results,
        [rows, *ups, *downs],
        [pltpu.VMEM(r.shape, r.dtype) for r in results]
        + [pltpu.VMEM((ROWS, WIDTH), bf16)] * 2
        + [pltpu.VMEM((RING, GROUP, WIDTH), bf16)] * 2
        + [pltpu.VMEM((RING, GROUP, ROWS), dtype) for dtype in (bf16, f32)]
        + [pltpu.SemaphoreType.DMA((2 * COLUMN + 2 * RING,))]
        + [pltpu.SemaphoreType.DMA((2 * RING + 1,))],
        flops=40 * ROWS * GROUP * WIDTH,
        limit=LARGE,
        outside=range(9),
        outputs_outside=True,
    )
    arrived = along_z(partial)
    far_up, far_down, left_up, left_down, right_up, right_down, own_up, own_down = gradients
    up_two, down_two = lax.optimization_barrier((along_x(far_up, 1), along_x(far_down, -1)))
    up_one = along_x(left_up, -1)
    down_one = along_x(right_down, 1)
    up_sum = along_x((right_up.astype(f32) + up_two.astype(f32)).astype(bf16), 1)
    down_sum = along_x((left_down.astype(f32) + down_two.astype(f32)).astype(bf16), -1)
    exponent = (LAYERS - 1 - layer_index).astype(f32)
    factor = jnp.power(f32(DECAY_RATE), exponent)
    step_up, step_down = call(
        step_kernel,
        [weight, weight],
        [
            factor,
            *(first_up[0].T, second_up[0].T, up_own, own_up, up_one, up_sum),
            *(first_down[0], second_down[0], down_own, own_down, down_one, down_sum),
        ],
        [pltpu.VMEM((2, 6, GROUP, WIDTH), bf16), pltpu.VMEM((2, GROUP, WIDTH), bf16)]
        + [pltpu.SemaphoreType.DMA((12,)), pltpu.SemaphoreType.DMA((2,))],
        limit=LARGE,
        outside=range(1, 13),
        outputs_outside=True,
    )

    scratch = [pltpu.VMEM((2 * CHUNK, WIDTH), bf16)]
    (summed,) = call(gather_kernel, [shape(SOURCES, 5 * FROM_ONE, 256)], [arrived], scratch)
    combined, gate_grad = call(
        combine_kernel,
        [shape(tokens.shape[0], WIDTH), shape(PICKS, 1, EXPERTS, dtype=f32)],
        [within_z(summed), cotangent, chosen, gates],
        [pltpu.VMEM((SOURCES * PADDED, WIDTH), f32)],
    )
    return (combined, gate_grad.transpose(1, 2, 0), step_up.T[None], step_down[None])


def solution(mesh):
    fine = Mesh(mesh.devices.reshape(4, RING, 2, 8, 2), ("zlo", "x", "zhi", "y", "core"))
    dp, expert = ("zlo", "x"), ("zhi", "y", "core")
    both = dp + expert
    placed = (
        P(both, None),
        P(both, None),
        P(both, None, None),
        P(both, None, None),
        P(expert, None, dp),
        P(expert, dp, None),
        P(expert, None, dp),
        P(expert, dp, None),
        P(expert, None, dp),
        P(expert, dp, None),
        P(),
    )
    return jax.shard_map(
        per_device,
        mesh=fine,
        in_specs=placed,
        out_specs=(P(both, None), P(both, None, None), P(expert, None, dp), P(expert, dp, None)),
        check_vma=False,
    )
```

```python
import jax
import jax.numpy as jnp
from jax import lax
from jax.experimental import pallas as pl
from jax.experimental.pallas import tpu as pltpu
from jax.sharding import Mesh, PartitionSpec as P

LAYERS = 32
STEP_COUNT = 10

BETA_ONE = 0.9
BETA_TWO = 0.999
EPSILON = 1e-08
DECAY_RATE = 0.9
WEIGHT_DECAY = 0.1

RING = 4
COLUMN = 8
SOURCES = 16
PICKS = 3
EXPERTS = 32
FROM_ONE = 6
PADDED = 8
CHUNK = SOURCES * PICKS
WIDTH = 1280
GROUP = 224
ROWS = COLUMN * CHUNK
SMALL, MIDDLE, LARGE = 12 * 1024 * 1024, 52 * 1024 * 1024, 60 * 1024 * 1024


def adam_step(gradient, first_moment, second_moment, weight, factor):
    mean_scale = factor * (1.0 / (1.0 - BETA_ONE**STEP_COUNT))
    square_scale = 1.0 / (1.0 - BETA_TWO**STEP_COUNT)
    mean = (mean_scale * BETA_ONE) * first_moment.astype(jnp.float32)
    mean = mean + (mean_scale * (1.0 - BETA_ONE)) * gradient
    square = (square_scale * BETA_TWO) * second_moment.astype(jnp.float32)
    square = square + (square_scale * (1.0 - BETA_TWO)) * (gradient * gradient)
    decay = (factor * WEIGHT_DECAY) * weight.astype(jnp.float32)
    return (mean / (jnp.sqrt(square) + EPSILON) + decay).astype(jnp.bfloat16)


def contract(left, right, left_dim, right_dim):
    return lax.dot_general(
        left,
        right,
        (((left_dim,), (right_dim,)), ((), ())),
        preferred_element_type=jnp.float32,
    )


def call(kernel, shapes, args, scratch=(), flops=0, limit=SMALL, outside=(), outputs_outside=False):
    spec = pl.BlockSpec(memory_space=pltpu.VMEM)
    moved = sum(a.size * a.dtype.itemsize for a in args)
    moved += sum(s.size * s.dtype.itemsize for s in shapes)
    far = pl.BlockSpec(memory_space=pl.ANY)
    scalar = pl.BlockSpec(memory_space=pltpu.SMEM)
    return pl.pallas_call(
        kernel,
        out_shape=shapes,
        in_specs=[
            scalar if a.ndim == 1 else far if i in outside else spec for i, a in enumerate(args)
        ],
        out_specs=[far if outputs_outside else spec] * len(shapes),
        scratch_shapes=scratch,
        compiler_params=pltpu.CompilerParams(vmem_limit_bytes=limit),
        cost_estimate=pl.CostEstimate(flops=flops, bytes_accessed=moved, transcendentals=0),
    )(*args)


def slot_masks():
    shape = (SOURCES * PADDED, EXPERTS)
    row = lax.broadcasted_iota(jnp.int32, shape, 0)
    lane = lax.broadcasted_iota(jnp.int32, shape, 1)
    slot = row & 7
    half = jnp.where(slot >= PICKS, 1, 0)
    same = (lane == half * SOURCES + (row >> 3)) & (slot < FROM_ONE)
    return [same & (slot - PICKS * half == k) for k in range(PICKS)]


def row_values(masks, values_ref):
    column = None
    for k in range(PICKS):
        term = jnp.where(masks[k], values_ref[k].astype(jnp.float32), 0.0)
        term = jnp.sum(term, axis=1, keepdims=True)
        column = term if column is None else column + term
    return column


def row_choice(masks, chosen_ref, tokens):
    chosen = row_values(masks, chosen_ref).astype(jnp.int32)
    local = lax.broadcasted_iota(jnp.int32, (SOURCES * PADDED, tokens), 1)
    return chosen == local


def pick_kernel(tokens, cotangent, chosen, gates, send, token_rows, back_rows, sems):
    copies = [
        pltpu.make_async_copy(tokens, token_rows, sems.at[0]),
        pltpu.make_async_copy(cotangent, back_rows, sems.at[1]),
    ]
    for copy in copies:
        copy.start()
    masks = slot_masks()
    choice = row_choice(masks, chosen, tokens.shape[0]).astype(jnp.bfloat16)
    gate = row_values(masks, gates)
    copies[0].wait()
    picked = contract(choice, token_rows[...], 1, 0)
    copies[1].wait()
    scaled = gate * contract(choice, back_rows[...], 1, 0)
    for i in range(SOURCES):
        here = slice(i * PADDED, i * PADDED + FROM_ONE)
        for n in range(2):
            cut = slice(n * WIDTH // 2, (n + 1) * WIDTH // 2)
            first = 2 * n * FROM_ONE
            send[i, first : first + FROM_ONE] = picked[here, cut].astype(jnp.bfloat16)
            send[i, first + FROM_ONE : first + 2 * FROM_ONE] = scaled[here, cut].astype(jnp.bfloat16)


def spread_kernel(arrived, send, rows):
    rows[...] = jnp.zeros_like(rows)
    for i in range(SOURCES):
        for n in range(2):
            cut = slice(n * WIDTH // 2, (n + 1) * WIDTH // 2)
            part = slice(2 * n * FROM_ONE, 2 * (n + 1) * FROM_ONE)
            rows[i * 16 : i * 16 + 2 * FROM_ONE, cut] = arrived[i, part]
    shape = (2 * CHUNK, SOURCES * 16)
    after = lax.broadcasted_iota(jnp.int32, shape, 0)
    before = lax.broadcasted_iota(jnp.int32, shape, 1)
    second = jnp.where(after >= CHUNK, 1, 0)
    after = after - CHUNK * second
    slot = (before & 15) - FROM_ONE * second - (after >> 4)
    for half in range(2):
        order = ((before >> 4) == (after & 15)) & (slot == PICKS * half)
        ordered = contract(order.astype(jnp.bfloat16), rows[...], 1, 0)
        ordered = ordered.astype(jnp.bfloat16)
        for z in range(4):
            send[z * 2 + half] = ordered


def gather_kernel(arrived, send, total):
    for half in range(2):
        chunk = arrived[half].astype(jnp.float32)
        for z in range(1, 4):
            chunk = chunk + arrived[z * 2 + half].astype(jnp.float32)
        total[half * CHUNK : half * CHUNK + CHUNK, :] = chunk.astype(jnp.bfloat16)
    shape = (SOURCES * PADDED, 2 * CHUNK)
    after = lax.broadcasted_iota(jnp.int32, shape, 0)
    before = lax.broadcasted_iota(jnp.int32, shape, 1)
    half = jnp.where(before >= CHUNK, 1, 0)
    before = before - CHUNK * half
    order = ((before & 15) == (after >> 3)) & ((after & 7) == PICKS * half + (before >> 4))
    ordered = contract(order.astype(jnp.bfloat16), total[...], 1, 0)
    for i in range(SOURCES):
        chunk = ordered[i * PADDED : i * PADDED + FROM_ONE].astype(jnp.bfloat16)
        for n in range(5):
            send[i, n * FROM_ONE : (n + 1) * FROM_ONE] = chunk[:, n * 256 : (n + 1) * 256]


def start_all(pairs, sems, first=0):
    copies = []
    for n, (source, target) in enumerate(pairs, first):
        copies.append(pltpu.make_async_copy(source, target, sems.at[n]))
        copies[-1].start()
    return copies


def wait_all(copies):
    for copy in copies:
        copy.wait()


def row_copies(arrived, half, rows):
    cut = pl.ds(half * CHUNK, CHUNK)
    return [(arrived.at[j, cut], rows.at[pl.ds(j * CHUNK, CHUNK)]) for j in range(COLUMN)]


CUTS = [pl.ds(n, 256) for n in range(0, WIDTH, 256)]


def expert_kernel(arrived, *args):
    ups, downs, outs, staged = args[:4], args[4:8], args[8:17], args[17:26]
    rows, grads, up, down, units, slopes, sems, out_sems = args[26:]
    partial = 8
    pairs = row_copies(arrived, 0, rows)
    pairs += [(ups[i], up.at[i]) for i in range(RING)] + row_copies(arrived, 1, grads)
    pairs += [(downs[i], down.at[i]) for i in range(RING)]
    copies = start_all(pairs, sems)
    wait_all(copies[:COLUMN])
    for i in range(RING):
        copies[COLUMN + i].wait()
        pre = contract(up[i], rows[...], 1, 1)
        share = 0.5 * (1.0 + lax.erf(pre * 0.7071067811865476))
        units[i] = (pre * share).astype(jnp.bfloat16)
        slopes[i] = share + pre * (0.3989422804014327 * jnp.exp(-0.5 * pre * pre))
    wait_all(copies[COLUMN + RING :])
    writes = []
    for i in range(RING):
        back = (slopes[i] * contract(down[i], grads[...], 1, 1)).astype(jnp.bfloat16)
        here = slice(2 * i, 2 * i + 2)
        for cut in CUTS:
            for out, a, b in zip(staged[here], (back, units[i]), (rows, grads)):
                out[:, cut] = contract(a, b[:, cut], 1, 0).astype(jnp.bfloat16)
        writes += start_all(list(zip(staged[here], outs[here])), out_sems, len(writes))
    for cut in CUTS:
        total = contract(units[0], down[0, :, cut], 0, 0)
        for i in range(1, RING):
            total = total + contract(units[i], down[i, :, cut], 0, 0)
        for j in range(COLUMN):
            staged[partial][j, :, cut] = total[j * CHUNK : j * CHUNK + CHUNK].astype(jnp.bfloat16)
    wait_all(writes + start_all([(staged[partial], outs[partial])], out_sems, len(writes)))


def step_kernel(factor, *args):
    sources, outs, (held, staged, sems, out_sems) = args[:12], args[12:14], args[14:]
    parts = [sources[:6], sources[6:]]
    pairs = [(source, held.at[n, m]) for n in range(2) for m, source in enumerate(parts[n])]
    copies = start_all(pairs, sems)
    writes = []
    for n in range(2):
        wait_all(copies[6 * n : 6 * n + 6])
        for start in range(0, GROUP, 32):
            here = pl.ds(start, 32)
            first_moment, second_moment, weight, own, one, two = [held[n, m, here] for m in range(6)]
            gradient = own.astype(jnp.float32) + one.astype(jnp.float32) + two.astype(jnp.float32)
            staged[n, here] = adam_step(gradient, first_moment, second_moment, weight, factor[0])
        writes += start_all([(staged.at[n], outs[n])], out_sems, len(writes))
    wait_all(writes)


def combine_kernel(returned, cotangent, chosen, gates, combined, gate_grad, rows):
    tokens = cotangent.shape[0]
    rows[...] = jnp.zeros_like(rows)
    for i in range(SOURCES):
        for n in range(5):
            part = returned[i, n * FROM_ONE : (n + 1) * FROM_ONE]
            rows[i * PADDED : i * PADDED + FROM_ONE, n * 256 : (n + 1) * 256] = part
    masks = slot_masks()
    choice = row_choice(masks, chosen, tokens)
    gate = row_values(masks, gates)
    weighted = jnp.where(choice, gate, 0.0)
    total = None
    for _ in range(3):
        piece = weighted.astype(jnp.bfloat16)
        weighted = weighted - piece.astype(jnp.float32)
        term = contract(piece, rows[...], 0, 0)
        total = term if total is None else total + term
    combined[...] = total.astype(jnp.bfloat16)
    back = contract(choice.astype(jnp.bfloat16), cotangent[...], 1, 0)
    inner = jnp.sum(back * rows[...].astype(jnp.float32), axis=1, keepdims=True)
    for k in range(PICKS):
        gate_grad[k] = jnp.sum(jnp.where(masks[k], inner, 0.0), axis=0, keepdims=True)


def shape(*dims, dtype=jnp.bfloat16):
    return jax.ShapeDtypeStruct(dims, dtype)


def along_x(values, step):
    return lax.ppermute(values, "x", [(i, (i + step) % RING) for i in range(RING)])


def within_z(rows):
    return lax.all_to_all(rows, ("y", "core"), split_axis=0, concat_axis=0, tiled=True)


def along_z(rows):
    return lax.all_to_all(rows, ("zlo", "zhi"), split_axis=0, concat_axis=0, tiled=True)


def per_device(
    tokens,
    cotangent,
    chosen_rows,
    combine_weights,
    up_weight,
    down_weight,
    first_up,
    first_down,
    second_up,
    second_down,
    layer_index,
):
    chosen = chosen_rows.transpose(2, 0, 1)
    gates = combine_weights.transpose(2, 0, 1)
    up_own = up_weight[0].T
    down_own = down_weight[0]
    f32, bf16 = jnp.float32, jnp.bfloat16

    up_left, down_left = along_x(up_own, 1), along_x(down_own, 1)
    up_right, down_right = along_x(up_own, -1), along_x(down_own, -1)

    (send,) = call(
        pick_kernel,
        [shape(SOURCES, 4 * FROM_ONE, WIDTH // 2)],
        [tokens, cotangent, chosen, gates],
        [pltpu.VMEM(tokens.shape, bf16)] * 2 + [pltpu.SemaphoreType.DMA((2,))],
        limit=LARGE,
        outside=(0, 1),
    )
    (spread,) = call(
        spread_kernel,
        [shape(COLUMN, 2 * CHUNK, WIDTH)],
        [within_z(send)],
        [pltpu.VMEM((SOURCES * 16, WIDTH), bf16)],
    )
    rows = along_z(spread)

    ups = [along_x(up_left, 1), up_left, up_right, up_own]
    downs = [along_x(down_right, -1), down_left, down_right, down_own]
    weight = shape(GROUP, WIDTH)
    results = [weight] * 8 + [shape(COLUMN, CHUNK, WIDTH)]
    *gradients, partial = call(
        expert_kernel,
        results,
        [rows, *ups, *downs],
        [pltpu.VMEM(r.shape, r.dtype) for r in results]
        + [pltpu.VMEM((ROWS, WIDTH), bf16)] * 2
        + [pltpu.VMEM((RING, GROUP, WIDTH), bf16)] * 2
        + [pltpu.VMEM((RING, GROUP, ROWS), dtype) for dtype in (bf16, f32)]
        + [pltpu.SemaphoreType.DMA((2 * COLUMN + 2 * RING,))]
        + [pltpu.SemaphoreType.DMA((2 * RING + 1,))],
        flops=40 * ROWS * GROUP * WIDTH,
        limit=MIDDLE,
        outside=range(9),
        outputs_outside=True,
    )
    arrived = along_z(partial)
    far_up, far_down, left_up, left_down, right_up, right_down, own_up, own_down = gradients
    up_two, down_two = lax.optimization_barrier((along_x(far_up, 1), along_x(far_down, -1)))
    up_one = along_x(left_up, -1)
    down_one = along_x(right_down, 1)
    up_sum = along_x((right_up.astype(f32) + up_two.astype(f32)).astype(bf16), 1)
    down_sum = along_x((left_down.astype(f32) + down_two.astype(f32)).astype(bf16), -1)
    exponent = (LAYERS - 1 - layer_index).astype(f32)
    factor = jnp.power(f32(DECAY_RATE), exponent)
    step_up, step_down = call(
        step_kernel,
        [weight, weight],
        [
            factor,
            *(first_up[0].T, second_up[0].T, up_own, own_up, up_one, up_sum),
            *(first_down[0], second_down[0], down_own, own_down, down_one, down_sum),
        ],
        [pltpu.VMEM((2, 6, GROUP, WIDTH), bf16), pltpu.VMEM((2, GROUP, WIDTH), bf16)]
        + [pltpu.SemaphoreType.DMA((12,)), pltpu.SemaphoreType.DMA((2,))],
        limit=LARGE,
        outside=range(1, 13),
        outputs_outside=True,
    )

    scratch = [pltpu.VMEM((2 * CHUNK, WIDTH), bf16)]
    (summed,) = call(gather_kernel, [shape(SOURCES, 5 * FROM_ONE, 256)], [arrived], scratch)
    combined, gate_grad = call(
        combine_kernel,
        [shape(tokens.shape[0], WIDTH), shape(PICKS, 1, EXPERTS, dtype=f32)],
        [within_z(summed), cotangent, chosen, gates],
        [pltpu.VMEM((SOURCES * PADDED, WIDTH), bf16)],
    )
    return (combined, gate_grad.transpose(1, 2, 0), step_up.T[None], step_down[None])


def solution(mesh):
    fine = Mesh(mesh.devices.reshape(4, RING, 2, 8, 2), ("zlo", "x", "zhi", "y", "core"))
    dp, expert = ("zlo", "x"), ("zhi", "y", "core")
    both = dp + expert
    placed = (
        P(both, None),
        P(both, None),
        P(both, None, None),
        P(both, None, None),
        P(expert, None, dp),
        P(expert, dp, None),
        P(expert, None, dp),
        P(expert, dp, None),
        P(expert, None, dp),
        P(expert, dp, None),
        P(),
    )
    return jax.shard_map(
        per_device,
        mesh=fine,
        in_specs=placed,
        out_specs=(P(both, None), P(both, None, None), P(expert, None, dp), P(expert, dp, None)),
        check_vma=False,
    )
```

```python
import jax
import jax.numpy as jnp
from jax import lax
from jax.experimental import pallas as pl
from jax.experimental.pallas import tpu as pltpu
from jax.sharding import Mesh, PartitionSpec as P

LAYERS = 32
STEP_COUNT = 10

BETA_ONE = 0.9
BETA_TWO = 0.999
EPSILON = 1e-08
DECAY_RATE = 0.9
WEIGHT_DECAY = 0.1

RING = 4
COLUMN = 8
SOURCES = 16
PICKS = 3
EXPERTS = 32
FROM_ONE = 6
PADDED = 8
CHUNK = SOURCES * PICKS
WIDTH = 1280
GROUP = 224
ROWS = COLUMN * CHUNK
SMALL, MIDDLE, LARGE = 12 * 1024 * 1024, 52 * 1024 * 1024, 60 * 1024 * 1024


def adam_step(gradient, first_moment, second_moment, weight, factor):
    mean_scale = factor * (1.0 / (1.0 - BETA_ONE**STEP_COUNT))
    square_scale = 1.0 / (1.0 - BETA_TWO**STEP_COUNT)
    mean = (mean_scale * BETA_ONE) * first_moment.astype(jnp.float32)
    mean = mean + (mean_scale * (1.0 - BETA_ONE)) * gradient
    square = (square_scale * BETA_TWO) * second_moment.astype(jnp.float32)
    square = square + (square_scale * (1.0 - BETA_TWO)) * (gradient * gradient)
    decay = (factor * WEIGHT_DECAY) * weight.astype(jnp.float32)
    return (mean / (jnp.sqrt(square) + EPSILON) + decay).astype(jnp.bfloat16)


def contract(left, right, left_dim, right_dim):
    return lax.dot_general(
        left,
        right,
        (((left_dim,), (right_dim,)), ((), ())),
        preferred_element_type=jnp.float32,
    )


def call(kernel, shapes, args, scratch=(), flops=0, limit=SMALL, outside=(), outputs_outside=False):
    spec = pl.BlockSpec(memory_space=pltpu.VMEM)
    moved = sum(a.size * a.dtype.itemsize for a in args)
    moved += sum(s.size * s.dtype.itemsize for s in shapes)
    far = pl.BlockSpec(memory_space=pl.ANY)
    scalar = pl.BlockSpec(memory_space=pltpu.SMEM)
    return pl.pallas_call(
        kernel,
        out_shape=shapes,
        in_specs=[
            scalar if a.ndim == 1 else far if i in outside else spec for i, a in enumerate(args)
        ],
        out_specs=[far if outputs_outside else spec] * len(shapes),
        scratch_shapes=scratch,
        compiler_params=pltpu.CompilerParams(vmem_limit_bytes=limit),
        cost_estimate=pl.CostEstimate(flops=flops, bytes_accessed=moved, transcendentals=0),
    )(*args)


def slot_masks():
    shape = (SOURCES * PADDED, EXPERTS)
    row = lax.broadcasted_iota(jnp.int32, shape, 0)
    lane = lax.broadcasted_iota(jnp.int32, shape, 1)
    slot = row & 7
    half = jnp.where(slot >= PICKS, 1, 0)
    same = (lane == half * SOURCES + (row >> 3)) & (slot < FROM_ONE)
    return [same & (slot - PICKS * half == k) for k in range(PICKS)]


def row_values(masks, values_ref):
    column = None
    for k in range(PICKS):
        term = jnp.where(masks[k], values_ref[k].astype(jnp.float32), 0.0)
        term = jnp.sum(term, axis=1, keepdims=True)
        column = term if column is None else column + term
    return column


def row_choice(masks, chosen_ref, tokens):
    chosen = row_values(masks, chosen_ref).astype(jnp.int32)
    local = lax.broadcasted_iota(jnp.int32, (SOURCES * PADDED, tokens), 1)
    return chosen == local


def pick_kernel(tokens, cotangent, chosen, gates, send, token_rows, back_rows, sems):
    copies = [
        pltpu.make_async_copy(tokens, token_rows, sems.at[0]),
        pltpu.make_async_copy(cotangent, back_rows, sems.at[1]),
    ]
    for copy in copies:
        copy.start()
    masks = slot_masks()
    choice = row_choice(masks, chosen, tokens.shape[0]).astype(jnp.bfloat16)
    gate = row_values(masks, gates)
    copies[0].wait()
    picked = contract(choice, token_rows[...], 1, 0)
    copies[1].wait()
    scaled = gate * contract(choice, back_rows[...], 1, 0)
    for i in range(SOURCES):
        here = slice(i * PADDED, i * PADDED + FROM_ONE)
        for n in range(2):
            cut = slice(n * WIDTH // 2, (n + 1) * WIDTH // 2)
            first = 2 * n * FROM_ONE
            send[i, first : first + FROM_ONE] = picked[here, cut].astype(jnp.bfloat16)
            send[i, first + FROM_ONE : first + 2 * FROM_ONE] = scaled[here, cut].astype(jnp.bfloat16)


def spread_kernel(arrived, send, rows):
    rows[...] = jnp.zeros_like(rows)
    for i in range(SOURCES):
        for n in range(2):
            cut = slice(n * WIDTH // 2, (n + 1) * WIDTH // 2)
            part = slice(2 * n * FROM_ONE, 2 * (n + 1) * FROM_ONE)
            rows[i * 16 : i * 16 + 2 * FROM_ONE, cut] = arrived[i, part]
    shape = (2 * CHUNK, SOURCES * 16)
    after = lax.broadcasted_iota(jnp.int32, shape, 0)
    before = lax.broadcasted_iota(jnp.int32, shape, 1)
    second = jnp.where(after >= CHUNK, 1, 0)
    after = after - CHUNK * second
    slot = (before & 15) - FROM_ONE * second - (after >> 4)
    for half in range(2):
        order = ((before >> 4) == (after & 15)) & (slot == PICKS * half)
        ordered = contract(order.astype(jnp.bfloat16), rows[...], 1, 0)
        ordered = ordered.astype(jnp.bfloat16)
        for z in range(4):
            send[z * 2 + half] = ordered


def gather_kernel(arrived, send, total):
    for half in range(2):
        chunk = arrived[half].astype(jnp.float32)
        for z in range(1, 4):
            chunk = chunk + arrived[z * 2 + half].astype(jnp.float32)
        total[half * CHUNK : half * CHUNK + CHUNK, :] = chunk.astype(jnp.bfloat16)
    shape = (SOURCES * PADDED, 2 * CHUNK)
    after = lax.broadcasted_iota(jnp.int32, shape, 0)
    before = lax.broadcasted_iota(jnp.int32, shape, 1)
    half = jnp.where(before >= CHUNK, 1, 0)
    before = before - CHUNK * half
    order = ((before & 15) == (after >> 3)) & ((after & 7) == PICKS * half + (before >> 4))
    ordered = contract(order.astype(jnp.bfloat16), total[...], 1, 0)
    for i in range(SOURCES):
        chunk = ordered[i * PADDED : i * PADDED + FROM_ONE].astype(jnp.bfloat16)
        for n in range(5):
            send[i, n * FROM_ONE : (n + 1) * FROM_ONE] = chunk[:, n * 256 : (n + 1) * 256]


def start_all(pairs, sems, first=0):
    copies = []
    for n, (source, target) in enumerate(pairs, first):
        copies.append(pltpu.make_async_copy(source, target, sems.at[n]))
        copies[-1].start()
    return copies


def wait_all(copies):
    for copy in copies:
        copy.wait()


def row_copies(arrived, half, rows):
    cut = pl.ds(half * CHUNK, CHUNK)
    return [(arrived.at[j, cut], rows.at[pl.ds(j * CHUNK, CHUNK)]) for j in range(COLUMN)]


CUTS = [pl.ds(n, 256) for n in range(0, WIDTH, 256)]


def gradients(back_hidden, slope, units, rows, grads, up_out, down_out):
    back = (slope * back_hidden).astype(jnp.bfloat16)
    for cut in CUTS:
        for out, a, b in zip((up_out, down_out), (back, units), (rows, grads)):
            out[:, cut] = contract(a, b[:, cut], 1, 0).astype(jnp.bfloat16)


def expert_kernel(arrived, *args):
    ups, downs, outs, staged = args[:4], args[4:8], args[8:13], args[13:18]
    rows, grads, up, down, sems, out_sems = args[18:]
    up_far, down_far, units, slopes, partial = staged
    pairs = row_copies(arrived, 0, rows)
    pairs += [(ups[i], up.at[i]) for i in range(RING)] + row_copies(arrived, 1, grads)
    pairs += [(downs[i], down.at[i]) for i in range(RING)]
    copies = start_all(pairs, sems)
    wait_all(copies[:COLUMN])
    for i in range(RING):
        copies[COLUMN + i].wait()
        pre = contract(up[i], rows[...], 1, 1)
        share = 0.5 * (1.0 + lax.erf(pre * 0.7071067811865476))
        units[i] = (pre * share).astype(jnp.bfloat16)
        slopes[i] = share + pre * (0.3989422804014327 * jnp.exp(-0.5 * pre * pre))
    writes = start_all([(units, outs[2]), (slopes, outs[3])], out_sems)
    wait_all(copies[COLUMN + RING :])
    back_hidden = contract(down[0], grads[...], 1, 1)
    gradients(back_hidden, slopes[0], units[0], rows, grads, up_far, down_far)
    writes += start_all([(up_far, outs[0]), (down_far, outs[1])], out_sems, len(writes))
    for cut in CUTS:
        total = contract(units[0], down[0, :, cut], 0, 0)
        for i in range(1, RING):
            total = total + contract(units[i], down[i, :, cut], 0, 0)
        for j in range(COLUMN):
            partial[j, :, cut] = total[j * CHUNK : j * CHUNK + CHUNK].astype(jnp.bfloat16)
    wait_all(writes + start_all([(partial, outs[4])], out_sems, len(writes)))


def backward_kernel(arrived, *args):
    downs, (hidden, slope), outs, staged = args[:3], args[3:5], args[5:11], args[11:17]
    rows, grads, down, units, slopes, sems, out_sems = args[17:]
    copies = start_all(row_copies(arrived, 1, grads), sems)
    first = [(downs[0], down.at[0]), (slope.at[1], slopes.at[0]), (hidden.at[1], units.at[0])]
    pairs = first + row_copies(arrived, 0, rows)
    for i in (1, 2):
        pairs.append((downs[i], down.at[i]))
        pairs += [(slope.at[i + 1], slopes.at[i]), (hidden.at[i + 1], units.at[i])]
    copies += start_all(pairs, sems, len(copies))
    wait_all(copies[: COLUMN + 3])
    writes = []
    for i in range(3):
        if i:
            late = 2 * COLUMN + 3 * i
            wait_all(copies[late : late + 3])
        back_hidden = contract(down[i], grads[...], 1, 1)
        if not i:
            wait_all(copies[COLUMN + 3 : 2 * COLUMN + 3])
        here = slice(2 * i, 2 * i + 2)
        gradients(back_hidden, slopes[i], units[i], rows, grads, *staged[here])
        writes += start_all(list(zip(staged[here], outs[here])), out_sems, len(writes))
    wait_all(writes)


def step_kernel(factor, *args):
    sources, out, (held, staged, sems, out_sems) = args[:6], args[6], args[7:]
    copies = start_all([(source, held.at[n]) for n, source in enumerate(sources)], sems)
    wait_all(copies)
    half, writes = GROUP // 2, []
    for n in range(2):
        for start in range(n * half, (n + 1) * half, 16):
            here = pl.ds(start, 16)
            first_moment, second_moment, weight, own, one, two = [held[m, here] for m in range(6)]
            gradient = own.astype(jnp.float32) + one.astype(jnp.float32) + two.astype(jnp.float32)
            staged[here] = adam_step(gradient, first_moment, second_moment, weight, factor[0])
        part = pl.ds(n * half, half)
        writes += start_all([(staged.at[part], out.at[part])], out_sems, n)
    wait_all(writes)


def combine_kernel(returned, cotangent, chosen, gates, combined, gate_grad, rows):
    tokens = cotangent.shape[0]
    rows[...] = jnp.zeros_like(rows)
    for i in range(SOURCES):
        for n in range(5):
            part = returned[i, n * FROM_ONE : (n + 1) * FROM_ONE]
            rows[i * PADDED : i * PADDED + FROM_ONE, n * 256 : (n + 1) * 256] = part
    masks = slot_masks()
    choice = row_choice(masks, chosen, tokens)
    gate = row_values(masks, gates)
    weighted = jnp.where(choice, gate, 0.0)
    total = None
    for _ in range(3):
        piece = weighted.astype(jnp.bfloat16)
        weighted = weighted - piece.astype(jnp.float32)
        term = contract(piece, rows[...], 0, 0)
        total = term if total is None else total + term
    combined[...] = total.astype(jnp.bfloat16)
    back = contract(choice.astype(jnp.bfloat16), cotangent[...], 1, 0)
    inner = jnp.sum(back * rows[...].astype(jnp.float32), axis=1, keepdims=True)
    for k in range(PICKS):
        gate_grad[k] = jnp.sum(jnp.where(masks[k], inner, 0.0), axis=0, keepdims=True)


def shape(*dims, dtype=jnp.bfloat16):
    return jax.ShapeDtypeStruct(dims, dtype)


def along_x(values, step):
    return lax.ppermute(values, "x", [(i, (i + step) % RING) for i in range(RING)])


def within_z(rows):
    return lax.all_to_all(rows, ("y", "core"), split_axis=0, concat_axis=0, tiled=True)


def along_z(rows):
    return lax.all_to_all(rows, ("zlo", "zhi"), split_axis=0, concat_axis=0, tiled=True)


def per_device(
    tokens,
    cotangent,
    chosen_rows,
    combine_weights,
    up_weight,
    down_weight,
    first_up,
    first_down,
    second_up,
    second_down,
    layer_index,
):
    chosen = chosen_rows.transpose(2, 0, 1)
    gates = combine_weights.transpose(2, 0, 1)
    up_own = up_weight[0].T
    down_own = down_weight[0]
    f32, bf16 = jnp.float32, jnp.bfloat16

    up_left, down_left = along_x(up_own, 1), along_x(down_own, 1)
    up_right, down_right = along_x(up_own, -1), along_x(down_own, -1)

    (send,) = call(
        pick_kernel,
        [shape(SOURCES, 4 * FROM_ONE, WIDTH // 2)],
        [tokens, cotangent, chosen, gates],
        [pltpu.VMEM(tokens.shape, bf16)] * 2 + [pltpu.SemaphoreType.DMA((2,))],
        limit=LARGE,
        outside=(0, 1),
    )
    (spread,) = call(
        spread_kernel,
        [shape(COLUMN, 2 * CHUNK, WIDTH)],
        [within_z(send)],
        [pltpu.VMEM((SOURCES * 16, WIDTH), bf16)],
    )
    rows = along_z(spread)

    ups = [along_x(up_left, 1), up_left, up_right, up_own]
    downs = [along_x(down_right, -1), down_left, down_right, down_own]
    weight = shape(GROUP, WIDTH)
    products = ROWS * GROUP * WIDTH
    held = [shape(RING, GROUP, ROWS), shape(RING, GROUP, ROWS, dtype=f32)]
    results = [weight, weight, *held, shape(COLUMN, CHUNK, WIDTH)]
    far_up, far_down, hidden, slope, partial = call(
        expert_kernel,
        results,
        [rows, *ups, *downs],
        [pltpu.VMEM(r.shape, r.dtype) for r in results]
        + [pltpu.VMEM((ROWS, WIDTH), bf16)] * 2
        + [pltpu.VMEM((RING, GROUP, WIDTH), bf16)] * 2
        + [pltpu.SemaphoreType.DMA((2 * COLUMN + 2 * RING,)), pltpu.SemaphoreType.DMA((5,))],
        flops=22 * products,
        limit=MIDDLE,
        outside=range(9),
        outputs_outside=True,
    )
    arrived = along_z(partial)
    results = [weight] * 6
    left_up, left_down, right_up, right_down, own_up, own_down = call(
        backward_kernel,
        results,
        [rows, *downs[1:], hidden, slope],
        [pltpu.VMEM(r.shape, r.dtype) for r in results]
        + [pltpu.VMEM((ROWS, WIDTH), bf16)] * 2
        + [pltpu.VMEM((3, GROUP, WIDTH), bf16)]
        + [pltpu.VMEM((3, GROUP, ROWS), dtype) for dtype in (bf16, f32)]
        + [pltpu.SemaphoreType.DMA((2 * COLUMN + 9,)), pltpu.SemaphoreType.DMA((6,))],
        flops=18 * products,
        limit=LARGE,
        outside=range(6),
        outputs_outside=True,
    )
    up_two, down_two = lax.optimization_barrier((along_x(far_up, 1), along_x(far_down, -1)))
    up_one = along_x(left_up, -1)
    down_one = along_x(right_down, 1)
    up_sum = along_x((right_up.astype(f32) + up_two.astype(f32)).astype(bf16), 1)
    down_sum = along_x((left_down.astype(f32) + down_two.astype(f32)).astype(bf16), -1)
    scratch = [pltpu.VMEM((2 * CHUNK, WIDTH), bf16)]
    (summed,) = call(gather_kernel, [shape(SOURCES, 5 * FROM_ONE, 256)], [arrived], scratch)
    combined, gate_grad = call(
        combine_kernel,
        [shape(tokens.shape[0], WIDTH), shape(PICKS, 1, EXPERTS, dtype=f32)],
        [within_z(summed), cotangent, chosen, gates],
        [pltpu.VMEM((SOURCES * PADDED, WIDTH), bf16)],
    )
    up_one, combined = lax.optimization_barrier((up_one, combined))

    exponent = (LAYERS - 1 - layer_index).astype(f32)
    factor = jnp.power(f32(DECAY_RATE), exponent)
    steps = []
    for parts in (
        (first_up[0].T, second_up[0].T, up_own, own_up, up_one, up_sum),
        (first_down[0], second_down[0], down_own, own_down, down_one, down_sum),
    ):
        steps += call(
            step_kernel,
            [weight],
            [factor, *parts],
            [pltpu.VMEM((6, GROUP, WIDTH), bf16), pltpu.VMEM((GROUP, WIDTH), bf16)]
            + [pltpu.SemaphoreType.DMA((6,)), pltpu.SemaphoreType.DMA((2,))],
            limit=LARGE,
            outside=range(1, 7),
            outputs_outside=True,
        )
    step_up, step_down = steps

    return (combined, gate_grad.transpose(1, 2, 0), step_up.T[None], step_down[None])


def solution(mesh):
    fine = Mesh(mesh.devices.reshape(4, RING, 2, 8, 2), ("zlo", "x", "zhi", "y", "core"))
    dp, expert = ("zlo", "x"), ("zhi", "y", "core")
    both = dp + expert
    placed = (
        P(both, None),
        P(both, None),
        P(both, None, None),
        P(both, None, None),
        P(expert, None, dp),
        P(expert, dp, None),
        P(expert, None, dp),
        P(expert, dp, None),
        P(expert, None, dp),
        P(expert, dp, None),
        P(),
    )
    return jax.shard_map(
        per_device,
        mesh=fine,
        in_specs=placed,
        out_specs=(P(both, None), P(both, None, None), P(expert, None, dp), P(expert, dp, None)),
        check_vma=False,
    )
```

```python
import jax
import jax.numpy as jnp
from jax import lax
from jax.experimental import pallas as pl
from jax.experimental.pallas import tpu as pltpu
from jax.sharding import Mesh, PartitionSpec as P

LAYERS = 32
STEP_COUNT = 10

BETA_ONE = 0.9
BETA_TWO = 0.999
EPSILON = 1e-08
DECAY_RATE = 0.9
WEIGHT_DECAY = 0.1

RING = 4
COLUMN = 8
SOURCES = 16
PICKS = 3
EXPERTS = 32
FROM_ONE = 6
PADDED = 8
CHUNK = SOURCES * PICKS
WIDTH = 1280
GROUP = 224
ROWS = COLUMN * CHUNK
SMALL, MIDDLE, LARGE = 12 * 1024 * 1024, 52 * 1024 * 1024, 60 * 1024 * 1024


def adam_step(gradient, first_moment, second_moment, weight, factor):
    mean_scale = factor * (1.0 / (1.0 - BETA_ONE**STEP_COUNT))
    square_scale = 1.0 / (1.0 - BETA_TWO**STEP_COUNT)
    mean = (mean_scale * BETA_ONE) * first_moment.astype(jnp.float32)
    mean = mean + (mean_scale * (1.0 - BETA_ONE)) * gradient
    square = (square_scale * BETA_TWO) * second_moment.astype(jnp.float32)
    square = square + (square_scale * (1.0 - BETA_TWO)) * (gradient * gradient)
    decay = (factor * WEIGHT_DECAY) * weight.astype(jnp.float32)
    return (mean / (jnp.sqrt(square) + EPSILON) + decay).astype(jnp.bfloat16)


def contract(left, right, left_dim, right_dim, precision=None):
    return lax.dot_general(
        left,
        right,
        (((left_dim,), (right_dim,)), ((), ())),
        precision=precision,
        preferred_element_type=jnp.float32,
    )


def call(kernel, shapes, args, scratch=(), flops=0, limit=SMALL, outside=(), outputs_outside=False):
    spec = pl.BlockSpec(memory_space=pltpu.VMEM)
    moved = sum(a.size * a.dtype.itemsize for a in args)
    moved += sum(s.size * s.dtype.itemsize for s in shapes)
    far = pl.BlockSpec(memory_space=pl.ANY)
    scalar = pl.BlockSpec(memory_space=pltpu.SMEM)
    return pl.pallas_call(
        kernel,
        out_shape=shapes,
        in_specs=[
            scalar if a.ndim == 1 else far if i in outside else spec for i, a in enumerate(args)
        ],
        out_specs=[far if outputs_outside else spec] * len(shapes),
        scratch_shapes=scratch,
        compiler_params=pltpu.CompilerParams(vmem_limit_bytes=limit),
        cost_estimate=pl.CostEstimate(flops=flops, bytes_accessed=moved, transcendentals=0),
    )(*args)


def slot_masks():
    shape = (SOURCES * PADDED, EXPERTS)
    row = lax.broadcasted_iota(jnp.int32, shape, 0)
    lane = lax.broadcasted_iota(jnp.int32, shape, 1)
    slot = row & 7
    half = jnp.where(slot >= PICKS, 1, 0)
    same = (lane == half * SOURCES + (row >> 3)) & (slot < FROM_ONE)
    return [same & (slot - PICKS * half == k) for k in range(PICKS)]


def row_values(masks, values_ref):
    column = None
    for k in range(PICKS):
        term = jnp.where(masks[k], values_ref[k].astype(jnp.float32), 0.0)
        term = jnp.sum(term, axis=1, keepdims=True)
        column = term if column is None else column + term
    return column


def row_choice(masks, chosen_ref, tokens):
    chosen = row_values(masks, chosen_ref).astype(jnp.int32)
    local = lax.broadcasted_iota(jnp.int32, (SOURCES * PADDED, tokens), 1)
    return chosen == local


def pick_kernel(tokens, cotangent, chosen, gates, send, token_rows, back_rows, sems):
    copies = [
        pltpu.make_async_copy(tokens, token_rows, sems.at[0]),
        pltpu.make_async_copy(cotangent, back_rows, sems.at[1]),
    ]
    for copy in copies:
        copy.start()
    masks = slot_masks()
    choice = row_choice(masks, chosen, tokens.shape[0]).astype(jnp.bfloat16)
    gate = row_values(masks, gates)
    copies[0].wait()
    picked = contract(choice, token_rows[...], 1, 0)
    copies[1].wait()
    scaled = gate * contract(choice, back_rows[...], 1, 0)
    for i in range(SOURCES):
        here = slice(i * PADDED, i * PADDED + FROM_ONE)
        for n in range(2):
            cut = slice(n * WIDTH // 2, (n + 1) * WIDTH // 2)
            first = 2 * n * FROM_ONE
            send[i, first : first + FROM_ONE] = picked[here, cut].astype(jnp.bfloat16)
            send[i, first + FROM_ONE : first + 2 * FROM_ONE] = scaled[here, cut].astype(jnp.bfloat16)


def spread_kernel(arrived, send, rows):
    rows[...] = jnp.zeros_like(rows)
    for i in range(SOURCES):
        for n in range(2):
            cut = slice(n * WIDTH // 2, (n + 1) * WIDTH // 2)
            part = slice(2 * n * FROM_ONE, 2 * (n + 1) * FROM_ONE)
            rows[i * 16 : i * 16 + 2 * FROM_ONE, cut] = arrived[i, part]
    shape = (2 * CHUNK, SOURCES * 16)
    after = lax.broadcasted_iota(jnp.int32, shape, 0)
    before = lax.broadcasted_iota(jnp.int32, shape, 1)
    second = jnp.where(after >= CHUNK, 1, 0)
    after = after - CHUNK * second
    slot = (before & 15) - FROM_ONE * second - (after >> 4)
    for half in range(2):
        order = ((before >> 4) == (after & 15)) & (slot == PICKS * half)
        ordered = contract(order.astype(jnp.bfloat16), rows[...], 1, 0)
        ordered = ordered.astype(jnp.bfloat16)
        for z in range(4):
            send[z * 2 + half] = ordered


def gather_kernel(arrived, send, total):
    for half in range(2):
        chunk = arrived[half].astype(jnp.float32)
        for z in range(1, 4):
            chunk = chunk + arrived[z * 2 + half].astype(jnp.float32)
        total[half * CHUNK : half * CHUNK + CHUNK, :] = chunk.astype(jnp.bfloat16)
    shape = (SOURCES * PADDED, 2 * CHUNK)
    after = lax.broadcasted_iota(jnp.int32, shape, 0)
    before = lax.broadcasted_iota(jnp.int32, shape, 1)
    half = jnp.where(before >= CHUNK, 1, 0)
    before = before - CHUNK * half
    order = ((before & 15) == (after >> 3)) & ((after & 7) == PICKS * half + (before >> 4))
    ordered = contract(order.astype(jnp.bfloat16), total[...], 1, 0)
    for i in range(SOURCES):
        chunk = ordered[i * PADDED : i * PADDED + FROM_ONE].astype(jnp.bfloat16)
        for n in range(5):
            send[i, n * FROM_ONE : (n + 1) * FROM_ONE] = chunk[:, n * 256 : (n + 1) * 256]


def start_all(pairs, sems, first=0):
    copies = []
    for n, (source, target) in enumerate(pairs, first):
        copies.append(pltpu.make_async_copy(source, target, sems.at[n]))
        copies[-1].start()
    return copies


def wait_all(copies):
    for copy in copies:
        copy.wait()


def row_copies(arrived, half, rows):
    cut = pl.ds(half * CHUNK, CHUNK)
    return [(arrived.at[j, cut], rows.at[pl.ds(j * CHUNK, CHUNK)]) for j in range(COLUMN)]


CUTS = [pl.ds(n, 256) for n in range(0, WIDTH, 256)]


def gradients(back_hidden, slope, units, rows, grads, up_out, down_out):
    back = (slope * back_hidden).astype(jnp.bfloat16)
    for cut in CUTS:
        for out, a, b in zip((up_out, down_out), (back, units), (rows, grads)):
            out[:, cut] = contract(a, b[:, cut], 1, 0).astype(jnp.bfloat16)


def expert_kernel(arrived, *args):
    ups, downs, outs, staged = args[:4], args[4:8], args[8:13], args[13:18]
    rows, grads, up, down, sems, out_sems = args[18:]
    up_far, down_far, units, slopes, partial = staged
    pairs = row_copies(arrived, 0, rows)
    pairs += [(ups[i], up.at[i]) for i in range(RING)] + row_copies(arrived, 1, grads)
    pairs += [(downs[i], down.at[i]) for i in range(RING)]
    copies = start_all(pairs, sems)
    wait_all(copies[:COLUMN])
    for i in range(RING):
        copies[COLUMN + i].wait()
        pre = contract(up[i], rows[...], 1, 1)
        share = 0.5 * (1.0 + lax.erf(pre * 0.7071067811865476))
        units[i] = (pre * share).astype(jnp.bfloat16)
        slopes[i] = share + pre * (0.3989422804014327 * jnp.exp(-0.5 * pre * pre))
    writes = start_all([(units, outs[2]), (slopes, outs[3])], out_sems)
    wait_all(copies[COLUMN + RING :])
    back_hidden = contract(down[0], grads[...], 1, 1)
    gradients(back_hidden, slopes[0], units[0], rows, grads, up_far, down_far)
    writes += start_all([(up_far, outs[0]), (down_far, outs[1])], out_sems, len(writes))
    for cut in CUTS:
        total = contract(units[0], down[0, :, cut], 0, 0)
        for i in range(1, RING):
            total = total + contract(units[i], down[i, :, cut], 0, 0)
        for j in range(COLUMN):
            partial[j, :, cut] = total[j * CHUNK : j * CHUNK + CHUNK].astype(jnp.bfloat16)
    wait_all(writes + start_all([(partial, outs[4])], out_sems, len(writes)))


def backward_kernel(arrived, *args):
    downs, (hidden, slope), outs, staged = args[:3], args[3:5], args[5:11], args[11:17]
    rows, grads, down, units, slopes, sems, out_sems = args[17:]
    copies = start_all(row_copies(arrived, 1, grads), sems)
    first = [(downs[0], down.at[0]), (slope.at[1], slopes.at[0]), (hidden.at[1], units.at[0])]
    pairs = first + row_copies(arrived, 0, rows)
    for i in (1, 2):
        pairs.append((downs[i], down.at[i]))
        pairs += [(slope.at[i + 1], slopes.at[i]), (hidden.at[i + 1], units.at[i])]
    copies += start_all(pairs, sems, len(copies))
    wait_all(copies[: COLUMN + 3])
    writes = []
    for i in range(3):
        if i:
            late = 2 * COLUMN + 3 * i
            wait_all(copies[late : late + 3])
        back_hidden = contract(down[i], grads[...], 1, 1)
        if not i:
            wait_all(copies[COLUMN + 3 : 2 * COLUMN + 3])
        here = slice(2 * i, 2 * i + 2)
        gradients(back_hidden, slopes[i], units[i], rows, grads, *staged[here])
        writes += start_all(list(zip(staged[here], outs[here])), out_sems, len(writes))
    wait_all(writes)


def step_kernel(factor, *args):
    sources, out, (held, staged, sems, out_sems) = args[:6], args[6], args[7:]
    copies = start_all([(source, held.at[n]) for n, source in enumerate(sources)], sems)
    wait_all(copies)
    half, writes = GROUP // 2, []
    for n in range(2):
        for start in range(n * half, (n + 1) * half, 16):
            here = pl.ds(start, 16)
            first_moment, second_moment, weight, own, one, two = [held[m, here] for m in range(6)]
            gradient = own.astype(jnp.float32) + one.astype(jnp.float32) + two.astype(jnp.float32)
            staged[here] = adam_step(gradient, first_moment, second_moment, weight, factor[0])
        part = pl.ds(n * half, half)
        writes += start_all([(staged.at[part], out.at[part])], out_sems, n)
    wait_all(writes)


def combine_kernel(returned, cotangent, chosen, gates, combined, gate_grad, rows):
    tokens = cotangent.shape[0]
    rows[...] = jnp.zeros_like(rows)
    for i in range(SOURCES):
        for n in range(5):
            part = returned[i, n * FROM_ONE : (n + 1) * FROM_ONE]
            rows[i * PADDED : i * PADDED + FROM_ONE, n * 256 : (n + 1) * 256] = part
    masks = slot_masks()
    choice = row_choice(masks, chosen, tokens)
    gate = row_values(masks, gates)
    weighted = jnp.where(choice, gate, 0.0)
    total = None
    for _ in range(3):
        piece = weighted.astype(jnp.bfloat16)
        weighted = weighted - piece.astype(jnp.float32)
        term = contract(piece, rows[...], 0, 0)
        total = term if total is None else total + term
    combined[...] = total.astype(jnp.bfloat16)
    back = contract(choice.astype(jnp.bfloat16), cotangent[...], 1, 0)
    inner = jnp.sum(back * rows[...].astype(jnp.float32), axis=1, keepdims=True)
    for k in range(PICKS):
        gate_grad[k] = jnp.sum(jnp.where(masks[k], inner, 0.0), axis=0, keepdims=True)


def shape(*dims, dtype=jnp.bfloat16):
    return jax.ShapeDtypeStruct(dims, dtype)


def along_x(values, step):
    return lax.ppermute(values, "x", [(i, (i + step) % RING) for i in range(RING)])


def within_z(rows):
    return lax.all_to_all(rows, ("y", "core"), split_axis=0, concat_axis=0, tiled=True)


def along_z(rows):
    return lax.all_to_all(rows, ("zlo", "zhi"), split_axis=0, concat_axis=0, tiled=True)


def per_device(
    tokens,
    cotangent,
    chosen_rows,
    combine_weights,
    up_weight,
    down_weight,
    first_up,
    first_down,
    second_up,
    second_down,
    layer_index,
):
    chosen = chosen_rows.transpose(2, 0, 1)
    gates = combine_weights.transpose(2, 0, 1)
    up_own = up_weight[0].T
    down_own = down_weight[0]
    f32, bf16 = jnp.float32, jnp.bfloat16

    up_left, down_left = along_x(up_own, 1), along_x(down_own, 1)
    up_right, down_right = along_x(up_own, -1), along_x(down_own, -1)

    (send,) = call(
        pick_kernel,
        [shape(SOURCES, 4 * FROM_ONE, WIDTH // 2)],
        [tokens, cotangent, chosen, gates],
        [pltpu.VMEM(tokens.shape, bf16)] * 2 + [pltpu.SemaphoreType.DMA((2,))],
        limit=LARGE,
        outside=(0, 1),
    )
    (spread,) = call(
        spread_kernel,
        [shape(COLUMN, 2 * CHUNK, WIDTH)],
        [within_z(send)],
        [pltpu.VMEM((SOURCES * 16, WIDTH), bf16)],
    )
    rows = along_z(spread)

    ups = [along_x(up_left, 1), up_left, up_right, up_own]
    downs = [along_x(down_right, -1), down_left, down_right, down_own]
    weight = shape(GROUP, WIDTH)
    products = ROWS * GROUP * WIDTH
    held = [shape(RING, GROUP, ROWS), shape(RING, GROUP, ROWS, dtype=f32)]
    results = [weight, weight, *held, shape(COLUMN, CHUNK, WIDTH)]
    far_up, far_down, hidden, slope, partial = call(
        expert_kernel,
        results,
        [rows, *ups, *downs],
        [pltpu.VMEM(r.shape, r.dtype) for r in results]
        + [pltpu.VMEM((ROWS, WIDTH), bf16)] * 2
        + [pltpu.VMEM((RING, GROUP, WIDTH), bf16)] * 2
        + [pltpu.SemaphoreType.DMA((2 * COLUMN + 2 * RING,)), pltpu.SemaphoreType.DMA((5,))],
        flops=22 * products,
        limit=MIDDLE,
        outside=range(9),
        outputs_outside=True,
    )
    arrived = along_z(partial)
    results = [weight] * 6
    left_up, left_down, right_up, right_down, own_up, own_down = call(
        backward_kernel,
        results,
        [rows, *downs[1:], hidden, slope],
        [pltpu.VMEM(r.shape, r.dtype) for r in results]
        + [pltpu.VMEM((ROWS, WIDTH), bf16)] * 2
        + [pltpu.VMEM((3, GROUP, WIDTH), bf16)]
        + [pltpu.VMEM((3, GROUP, ROWS), dtype) for dtype in (bf16, f32)]
        + [pltpu.SemaphoreType.DMA((2 * COLUMN + 9,)), pltpu.SemaphoreType.DMA((6,))],
        flops=18 * products,
        limit=LARGE,
        outside=range(6),
        outputs_outside=True,
    )
    up_two, down_two = lax.optimization_barrier((along_x(far_up, 1), along_x(far_down, -1)))
    up_one = along_x(left_up, -1)
    down_one = along_x(right_down, 1)
    up_sum = along_x((right_up.astype(f32) + up_two.astype(f32)).astype(bf16), 1)
    down_sum = along_x((left_down.astype(f32) + down_two.astype(f32)).astype(bf16), -1)
    exponent = (LAYERS - 1 - layer_index).astype(f32)
    factor = jnp.power(f32(DECAY_RATE), exponent)
    steps = []
    for parts in (
        (first_up[0].T, second_up[0].T, up_own, own_up, up_one, up_sum),
        (first_down[0], second_down[0], down_own, own_down, down_one, down_sum),
    ):
        steps += call(
            step_kernel,
            [weight],
            [factor, *parts],
            [pltpu.VMEM((6, GROUP, WIDTH), bf16), pltpu.VMEM((GROUP, WIDTH), bf16)]
            + [pltpu.SemaphoreType.DMA((6,)), pltpu.SemaphoreType.DMA((2,))],
            limit=LARGE,
            outside=range(1, 7),
            outputs_outside=True,
        )
    step_up, step_down = steps

    scratch = [pltpu.VMEM((2 * CHUNK, WIDTH), bf16)]
    (summed,) = call(gather_kernel, [shape(SOURCES, 5 * FROM_ONE, 256)], [arrived], scratch)
    combined, gate_grad = call(
        combine_kernel,
        [shape(tokens.shape[0], WIDTH), shape(PICKS, 1, EXPERTS, dtype=f32)],
        [within_z(summed), cotangent, chosen, gates],
        [pltpu.VMEM((SOURCES * PADDED, WIDTH), bf16)],
    )
    return (combined, gate_grad.transpose(1, 2, 0), step_up.T[None], step_down[None])


def solution(mesh):
    fine = Mesh(mesh.devices.reshape(4, RING, 2, 8, 2), ("zlo", "x", "zhi", "y", "core"))
    dp, expert = ("zlo", "x"), ("zhi", "y", "core")
    both = dp + expert
    placed = (
        P(both, None),
        P(both, None),
        P(both, None, None),
        P(both, None, None),
        P(expert, None, dp),
        P(expert, dp, None),
        P(expert, None, dp),
        P(expert, dp, None),
        P(expert, None, dp),
        P(expert, dp, None),
        P(),
    )
    return jax.shard_map(
        per_device,
        mesh=fine,
        in_specs=placed,
        out_specs=(P(both, None), P(both, None, None), P(expert, None, dp), P(expert, dp, None)),
        check_vma=False,
    )
```
